32 devices in a mesh: frame: 4 (over y, x), tile: 8 (over z, core).
Axes of the slice: x: 2, y: 2, z: 4, core: 2. Of those that a mesh axis runs over, the one named last changes fastest.
Arguments:
- latents: bfloat16 [4, 320, 2048], P('frame', None, 'tile'), may hold values from -80 to 80
- out_grad: bfloat16 [4, 320, 2048], P('frame', None, 'tile'), may hold values from -6 to 6
- w_spatial: bfloat16 [320, 2880], P('tile', 'frame'), may hold values from -0.109375 to 0.109375
- w_temporal: bfloat16 [320, 960], P('tile', 'frame'), may hold values from -0.1875 to 0.1875
- norm_gain: float32 [320], replicated, may hold values from 0.5 to 1.5
- norm_shift: float32 [320], replicated, may hold values from -1 to 1
- heights: int32 [8], P('tile'), may hold values from 8 to 16, as said below
Outputs:
- grad_input: bfloat16 [4, 320, 2048], P('frame', None, 'tile')
- grad_spatial: float32 [320, 2880], P('tile', 'frame')
- grad_temporal: float32 [320, 960], P('tile', 'frame')
- grad_gain: float32 [320], replicated
- grad_shift: float32 [320], replicated
The draws below stay inside these ranges and needn't reach their ends.
Inputs may be any that keep to these rules, and one draw needn't show every extreme that they name: `heights`: each entry is a multiple of 8; in every draw at least one strip has 16 live rows.
All inputs are finite; a program needn't handle non-finite values.
Results may differ from the reference program's by a relative error of at most 0.028.
Values may be sent and summed in bfloat16 or wider, within the bound.
A program may use at most 64 MiB of HBM per device.

```python
import jax
import jax.numpy as jnp
from jax import lax

CHANNELS = 320
GROUPS = 32
COLUMNS = 16
STRIP_ROWS = 16
FRAMES = 4
STRIPS = 8
PIXELS = 2048


def draw_latents(key, part):
    key_base, key_scale, key_offset = jax.random.split(key, 3)
    frame_pos = jnp.arange(FRAMES, dtype=jnp.float32) / max(FRAMES - 1, 1)
    strip_pos = (jnp.arange(PIXELS, dtype=jnp.int32) // (STRIP_ROWS * COLUMNS)).astype(jnp.float32) / max(STRIPS - 1, 1)
    chan_scale = jnp.exp(jax.random.uniform(key_scale, (CHANNELS,), jnp.float32, jnp.log(0.4), jnp.log(4.0)))
    offset = jax.random.uniform(key_offset, (CHANNELS,), jnp.float32, -1.0, 1.0)
    base = jnp.clip(jax.random.normal(key_base, (FRAMES, CHANNELS, PIXELS), jnp.float32), -6.0, 6.0)
    rise = 1.0 + frame_pos[:, None, None] + strip_pos[None, None, :]
    values = offset[None, :, None] + chan_scale[None, :, None] * rise * base
    return values.astype(jnp.bfloat16)


def draw_heights(key, part):
    key_tall, key_pick = jax.random.split(key)
    tall_strip = jax.random.randint(key_tall, (STRIPS,), 0, 8) == 0
    chosen = jax.random.randint(key_pick, (), 0, STRIPS)
    tall_strip = tall_strip | (jnp.arange(STRIPS, dtype=jnp.int32) == chosen)
    return jnp.where(tall_strip, STRIP_ROWS, 8).astype(jnp.int32)


def raised(entries, key, source, target, shards_of, factor):
    def block_of(dim):
        return (jnp.arange(entries.shape[dim]) // (entries.shape[dim] // shards_of)).reshape((-1,) + (1,) * (entries.ndim - 1 - dim))

    first = jax.random.permutation(key, shards_of)[block_of(target)]
    second = (block_of(target) + shards_of // 2) % shards_of
    return jnp.where((block_of(source) == first) | (block_of(source) == second), factor * entries, entries)


def level_of(own_key, shape, cuts, smallest, high):
    factor_of = 1.0
    for dim, parts in cuts:
        steps = jax.random.uniform(jax.random.fold_in(jax.random.fold_in(own_key, 6), dim), (parts,), jnp.float32, smallest / len(cuts), high / len(cuts))
        factor_of = factor_of * jnp.repeat(jnp.exp(steps), shape[dim] // parts).reshape((-1,) + (1,) * (len(shape) - 1 - dim))
    return factor_of


def gaussian(key, extent, spread, limit, cuts=(), kind=jnp.bfloat16):
    gain = level_of(key, extent, cuts, -0.22, 0.18) if cuts else 1.0
    array = jax.random.normal(key, extent, jnp.float32) * spread * gain
    return jnp.minimum(jnp.maximum(array, -limit), limit).astype(kind)


def heavy_noise(key, dims, scale, bound, cuts, heavy, held_as=jnp.bfloat16):
    entries = scale * jax.random.normal(key, dims, jnp.float32)
    if cuts:
        entries = entries * level_of(key, dims, cuts, -0.22, 0.18)
    return jnp.clip(raised(entries, jax.random.fold_in(key, 3), *heavy), -bound, bound).astype(held_as)


def setup_inputs(seed: int = 0) -> dict:
    key_of = jax.random.split(jax.random.key(seed), 8)
    latents = draw_latents(jax.random.fold_in(key_of[7], 71), 0)
    out_grad = heavy_noise(key_of[1], (FRAMES, CHANNELS, PIXELS), 1.0, 6.0, ((0, 4), (2, 8)), (2, 1, 8, 2.0))
    w_spatial = gaussian(key_of[2], (CHANNELS, 9 * CHANNELS), (9 * CHANNELS) ** -0.5, 0.109375, ((0, 8), (1, 4)))
    w_temporal = gaussian(key_of[3], (CHANNELS, 3 * CHANNELS), (3 * CHANNELS) ** -0.5, 0.1875, ((0, 8), (1, 4)))
    norm_gain = jnp.clip(jax.random.uniform(key_of[4], (CHANNELS,), jnp.float32, 0.5, 1.5), 0.5, 1.5)
    norm_shift = jnp.clip(jax.random.uniform(key_of[5], (CHANNELS,), jnp.float32, -1.0, 1.0), -1.0, 1.0)
    heights = draw_heights(jax.random.fold_in(key_of[7], 71), 0)
    return {"latents": latents, "out_grad": out_grad, "w_spatial": w_spatial, "w_temporal": w_temporal, "norm_gain": norm_gain, "norm_shift": norm_shift, "heights": heights}


EPSILON = 1e-05

def neighbor_tables(heights):
    slot_index = jnp.arange(STRIPS * STRIP_ROWS, dtype=jnp.int32)
    strip_index = slot_index // STRIP_ROWS
    row_within = slot_index % STRIP_ROWS
    own_height = heights[strip_index]
    previous_height = heights[jnp.maximum(strip_index - 1, 0)]
    live_rows = row_within < own_height
    above_index = jnp.where(row_within > 0, slot_index - 1, (strip_index - 1) * STRIP_ROWS + previous_height - 1)
    above_valid = live_rows & ((row_within > 0) | (strip_index > 0))
    below_index = jnp.where(row_within + 1 < own_height, slot_index + 1, (strip_index + 1) * STRIP_ROWS)
    below_valid = live_rows & ((row_within + 1 < own_height) | (strip_index < STRIPS - 1))
    last_slot = STRIPS * STRIP_ROWS - 1
    return (live_rows, jnp.clip(above_index, 0, last_slot), above_valid, jnp.clip(below_index, 0, last_slot), below_valid)

def spatial_columns(field_grid, tables):
    live_rows, above_index, above_valid, below_index, below_valid = tables
    zero_value = jnp.zeros((), field_grid.dtype)
    upper_rows = jnp.where(above_valid[None, :, None], jnp.take(field_grid, above_index, axis=1), zero_value)
    lower_rows = jnp.where(below_valid[None, :, None], jnp.take(field_grid, below_index, axis=1), zero_value)
    pieces = []
    for rows_here in (upper_rows, field_grid, lower_rows):
        padded = jnp.pad(rows_here, ((0, 0), (0, 0), (1, 1)))
        for col_step in range(3):
            pieces.append(padded[:, :, col_step:col_step + COLUMNS])
    stacked = jnp.stack(pieces, axis=0)
    return stacked.reshape(9 * field_grid.shape[0], field_grid.shape[1] * COLUMNS)

def flip_taps(weight, tap_count):
    outputs = weight.shape[0]
    return jnp.transpose(weight.reshape(outputs, tap_count, -1)[:, ::-1, :], (2, 1, 0)).reshape(-1, tap_count * outputs)

def strip_partials(left_side, right_side):
    left_strips = left_side.astype(jnp.float32).reshape(left_side.shape[0], STRIPS, -1)
    right_strips = right_side.astype(jnp.float32).reshape(right_side.shape[0], STRIPS, -1)
    strip_parts = jnp.einsum('otp,ktp->tok', left_strips, right_strips, precision=lax.Precision.HIGHEST)
    rounded = lax.optimization_barrier(strip_parts.astype(jnp.bfloat16))
    return lax.optimization_barrier(jnp.sum(rounded.astype(jnp.float32), axis=0))

def reference(latents, out_grad, w_spatial, w_temporal, norm_gain, norm_shift, heights):
    tables = neighbor_tables(heights)
    live_cells = jnp.repeat(tables[0], COLUMNS)
    live_float = live_cells.astype(jnp.float32)
    group_size = CHANNELS // GROUPS
    rows_total = STRIPS * STRIP_ROWS
    latent_full = latents.astype(jnp.float32)
    masked = latent_full * live_float[None, None, :]
    chan_sum = lax.optimization_barrier(jnp.sum(masked, axis=(0, 2)))
    chan_square = lax.optimization_barrier(jnp.sum(masked * latent_full, axis=(0, 2)))
    position_count = FRAMES * jnp.sum(heights).astype(jnp.float32) * COLUMNS
    group_count = position_count * group_size
    group_mean = chan_sum.reshape(GROUPS, group_size).sum(1) / group_count
    group_var = chan_square.reshape(GROUPS, group_size).sum(1) / group_count - group_mean * group_mean
    group_rstd = lax.rsqrt(group_var + EPSILON)
    mean_column = jnp.repeat(group_mean, group_size)[:, None]
    rstd_column = jnp.repeat(group_rstd, group_size)[:, None]
    gain_column = norm_gain.astype(jnp.float32)[:, None]
    shift_column = norm_shift.astype(jnp.float32)[:, None]

    def frame_norm(frame_latent):
        normed = (frame_latent.astype(jnp.float32) - mean_column) * rstd_column
        pre_act = gain_column * normed + shift_column
        activated = jnp.where(live_cells[None, :], jax.nn.silu(pre_act), 0.0).astype(jnp.bfloat16)
        return (normed, pre_act, activated)

    def frame_forward(frame_latent):
        activated = frame_norm(frame_latent)[2]
        columns_here = spatial_columns(activated.reshape(CHANNELS, rows_total, COLUMNS), tables)
        spatial_raw = jnp.dot(w_spatial, columns_here, preferred_element_type=jnp.float32)
        return jnp.where(live_cells[None, :], spatial_raw, 0.0).astype(jnp.bfloat16)
    spatial_out = lax.map(frame_forward, latents)
    grad_masked = jnp.where(live_cells[None, None, :], out_grad, jnp.zeros((), jnp.bfloat16))
    zero_frame = jnp.zeros((1, CHANNELS, PIXELS), jnp.bfloat16)
    spatial_pad = jnp.concatenate([zero_frame, spatial_out, zero_frame], axis=0)
    grad_pad = jnp.concatenate([zero_frame, grad_masked, zero_frame], axis=0)
    temporal_flip = flip_taps(w_temporal, 3)
    spatial_flip = flip_taps(w_spatial, 9)

    def frame_backward(running, frame_index):
        sum_spatial, sum_temporal, sum_gain, sum_shift = running
        frame_latent = lax.dynamic_index_in_dim(latents, frame_index, 0, keepdims=False)
        normed, pre_act, activated = frame_norm(frame_latent)
        act_columns = spatial_columns(activated.reshape(CHANNELS, rows_total, COLUMNS), tables)
        grad_frame = lax.dynamic_index_in_dim(grad_masked, frame_index, 0, keepdims=False)
        spat_window = lax.dynamic_slice_in_dim(spatial_pad, frame_index, 3, 0).reshape(3 * CHANNELS, PIXELS)
        grad_window = lax.dynamic_slice_in_dim(grad_pad, frame_index, 3, 0).reshape(3 * CHANNELS, PIXELS)
        grad_spat = jnp.dot(temporal_flip, grad_window, preferred_element_type=jnp.float32)
        grad_spat = jnp.where(live_cells[None, :], grad_spat, 0.0).astype(jnp.bfloat16)
        grad_columns = spatial_columns(grad_spat.reshape(CHANNELS, rows_total, COLUMNS), tables)
        grad_act = jnp.dot(spatial_flip, grad_columns, preferred_element_type=jnp.float32)
        sigmoid_act = jax.nn.sigmoid(pre_act)
        grad_pre = jnp.where(live_cells[None, :], grad_act * sigmoid_act * (1.0 + pre_act * (1.0 - sigmoid_act)), 0.0)
        sum_temporal = sum_temporal + strip_partials(grad_frame, spat_window)
        sum_spatial = sum_spatial + strip_partials(grad_spat, act_columns)
        sum_gain = sum_gain + lax.optimization_barrier(jnp.sum(grad_pre * normed, axis=1))
        sum_shift = sum_shift + lax.optimization_barrier(jnp.sum(grad_pre, axis=1))
        return ((sum_spatial, sum_temporal, sum_gain, sum_shift), grad_pre)
    start = (jnp.zeros((CHANNELS, 9 * CHANNELS), jnp.float32), jnp.zeros((CHANNELS, 3 * CHANNELS), jnp.float32), jnp.zeros((CHANNELS,), jnp.float32), jnp.zeros((CHANNELS,), jnp.float32))
    finals, grad_pre_all = lax.scan(frame_backward, start, jnp.arange(FRAMES, dtype=jnp.int32))
    sum_spatial, sum_temporal, chan_gain, chan_shift = finals
    shift_sum = (norm_gain * chan_shift).reshape(GROUPS, group_size).sum(1) / group_count
    gain_sum = (norm_gain * chan_gain).reshape(GROUPS, group_size).sum(1) / group_count
    shift_column_sum = jnp.repeat(shift_sum, group_size)[:, None]
    gain_column_sum = jnp.repeat(gain_sum, group_size)[:, None]

    def frame_input(pair):
        frame_latent, grad_pre, grad_frame = pair
        normed = (frame_latent.astype(jnp.float32) - mean_column) * rstd_column
        result = grad_frame.astype(jnp.float32) + rstd_column * (gain_column * grad_pre - shift_column_sum - normed * gain_column_sum)
        return jnp.where(live_cells[None, :], result, 0.0).astype(jnp.bfloat16)
    grad_input = lax.map(frame_input, (latents, grad_pre_all, grad_masked))
    grad_scale = lax.rsqrt(position_count)
    return (grad_input, grad_scale * sum_spatial, grad_scale * sum_temporal, grad_scale * chan_gain, grad_scale * chan_shift)
```

```python
import jax
import jax.numpy as jnp
from jax import lax
from jax.experimental import pallas as pl
from jax.experimental.pallas import tpu as pltpu
from jax.sharding import PartitionSpec as P

GROUPS = 32
COLUMNS = 16
STRIP_ROWS = 16


EPSILON = 1e-05


def from_behind(shard, axis, by):
    peers = lax.axis_size(axis)
    pairs = [(i, i + by) for i in range(peers) if 0 <= i + by < peers]
    return lax.ppermute(shard, axis, pairs)


def padded_2(cells, sides, width):
    for axis, dim in sides:
        count = lax.axis_size(axis)
        ends = count - 1
        head = lax.slice_in_dim(cells, 0, width, axis=dim)
        tail = lax.slice_in_dim(cells, cells.shape[dim] - width, cells.shape[dim], axis=dim)
        cells = jnp.concatenate(
            [
                lax.ppermute(tail, axis, [(i, (i + 1) % count) for i in range(ends)]),
                cells,
                lax.ppermute(head, axis, [((i + 1) % count, i) for i in range(ends)]),
            ],
            axis=dim,
        )
    return cells


def flip_taps(weight, tap_count):
    outputs = weight.shape[0]
    return jnp.transpose(weight.reshape(outputs, tap_count, -1)[:, ::-1, :], (2, 1, 0)).reshape(
        -1, tap_count * outputs
    )


def padded_rows(row_grid, above_row, below_row, height):
    channel_count = row_grid.shape[0]
    padded = jnp.zeros((channel_count, STRIP_ROWS + 2, COLUMNS + 2), row_grid.dtype)
    padded = padded.at[:, 1 : STRIP_ROWS + 1, 1 : COLUMNS + 1].set(row_grid)
    padded = padded.at[:, 0, 1 : COLUMNS + 1].set(above_row)
    below_block = jnp.pad(below_row, ((0, 0), (1, 1)))[:, None, :]
    return lax.dynamic_update_slice(padded, below_block, (jnp.int32(0), height + 1, jnp.int32(0)))


def tap_columns(padded, row_count):
    pieces = [
        padded[:, row_step : row_step + row_count, col_step : col_step + COLUMNS]
        for row_step in range(3)
        for col_step in range(3)
    ]
    return jnp.stack(pieces, axis=0).reshape(9 * padded.shape[0], row_count * COLUMNS)


def local(latents, out_grad, w_spatial, w_temporal, norm_gain, norm_shift, heights):
    channel_count = latents.shape[1]
    cell_count = latents.shape[2]
    group_size = channel_count // GROUPS
    height = heights[0]
    slot_row = jnp.arange(cell_count, dtype=jnp.int32) // COLUMNS
    live_cells = slot_row < height
    live_float = live_cells.astype(jnp.float32)
    contract_last = (((1,), (1,)), ((), ()))
    part_spatial_w, part_temporal_w = (
        lax.all_gather(w_spatial, "frame", axis=1, tiled=True),
        lax.all_gather(w_temporal, "frame", axis=1, tiled=True),
    )
    spatial_full, temporal_full = (
        lax.all_gather(part_spatial_w, "tile", axis=0, tiled=True),
        lax.all_gather(part_temporal_w, "tile", axis=0, tiled=True),
    )
    latent_full = latents[0].astype(jnp.float32)
    masked = latent_full * live_float[None, :]
    group_sum = masked.reshape(GROUPS, group_size, cell_count).sum(axis=(1, 2))
    group_square = (masked * latent_full).reshape(GROUPS, group_size, cell_count).sum(axis=(1, 2))
    own_count = height.astype(jnp.float32) * COLUMNS
    total_sum, total_square, position_count = lax.psum(
        (group_sum, group_square, own_count), ("frame", "tile")
    )
    group_count = position_count * group_size
    group_mean = total_sum / group_count
    group_rstd = lax.rsqrt(total_square / group_count - group_mean * group_mean + EPSILON)
    mean_column = jnp.repeat(group_mean, group_size)[:, None]
    rstd_column = jnp.repeat(group_rstd, group_size)[:, None]
    gain_column = norm_gain[:, None]
    normed = (latent_full - mean_column) * rstd_column
    pre_act = gain_column * normed + norm_shift[:, None]
    activated = jnp.where(live_cells[None, :], jax.nn.silu(pre_act), 0.0).astype(jnp.bfloat16)
    act_grid = activated.reshape(channel_count, STRIP_ROWS, COLUMNS)
    last_live = lax.dynamic_slice_in_dim(act_grid, height - 1, 1, 1)[:, 0, :]
    from_above = from_behind(last_live, "tile", 1)
    from_below = from_behind(act_grid[:, 0, :], "tile", -1)
    act_padded = padded_rows(act_grid, from_above, from_below, height)
    act_columns = tap_columns(act_padded, STRIP_ROWS)
    spatial_raw = jnp.dot(spatial_full, act_columns, preferred_element_type=jnp.float32)
    spatial_out = jnp.where(live_cells[None, :], spatial_raw, 0.0).astype(jnp.bfloat16)
    spatial_frames = padded_2(spatial_out[None], (("frame", 0),), 1)
    grad_here = jnp.where(live_cells[None, :], out_grad[0], jnp.zeros((), jnp.bfloat16))
    grad_frames = padded_2(grad_here[None], (("frame", 0),), 1)
    part_temporal = lax.dot_general(
        grad_here,
        spatial_frames.reshape(3 * channel_count, cell_count),
        contract_last,
        preferred_element_type=jnp.float32,
    )
    grad_spat = jnp.dot(
        flip_taps(temporal_full, 3),
        grad_frames.reshape(3 * channel_count, cell_count),
        preferred_element_type=jnp.float32,
    )
    grad_spat = jnp.where(live_cells[None, :], grad_spat, 0.0).astype(jnp.bfloat16)
    spat_grid = grad_spat.reshape(channel_count, STRIP_ROWS, COLUMNS)
    grad_last = lax.dynamic_slice_in_dim(spat_grid, height - 1, 1, 1)[:, 0, :]
    grad_above = from_behind(grad_last, "tile", 1)
    grad_below = from_behind(spat_grid[:, 0, :], "tile", -1)
    grad_padded = padded_rows(spat_grid, grad_above, grad_below, height)
    spatial_flip = flip_taps(spatial_full, 9)
    grad_act = jnp.dot(
        spatial_flip, tap_columns(grad_padded, STRIP_ROWS), preferred_element_type=jnp.float32
    )
    part_spatial = lax.dot_general(
        grad_spat, act_columns, contract_last, preferred_element_type=jnp.float32
    )
    sigmoid_act = jax.nn.sigmoid(pre_act)
    grad_pre = jnp.where(
        live_cells[None, :], grad_act * sigmoid_act * (1.0 + pre_act * (1.0 - sigmoid_act)), 0.0
    )
    chan_gain, chan_shift = lax.psum(
        (jnp.sum(grad_pre * normed, axis=1), jnp.sum(grad_pre, axis=1)), ("frame", "tile")
    )
    shift_sum = (norm_gain * chan_shift).reshape(GROUPS, group_size).sum(1) / group_count
    gain_sum = (norm_gain * chan_gain).reshape(GROUPS, group_size).sum(1) / group_count
    result = grad_here.astype(jnp.float32) + rstd_column * (
        gain_column * grad_pre
        - jnp.repeat(shift_sum, group_size)[:, None]
        - normed * jnp.repeat(gain_sum, group_size)[:, None]
    )
    grad_input = jnp.where(live_cells[None, :], result, 0.0).astype(jnp.bfloat16)[None]
    tile_spatial, tile_temporal = (
        lax.psum_scatter(
            part_spatial.astype(jnp.bfloat16), "tile", scatter_dimension=0, tiled=True
        ).astype(jnp.float32),
        lax.psum_scatter(
            part_temporal.astype(jnp.bfloat16), "tile", scatter_dimension=0, tiled=True
        ).astype(jnp.float32),
    )
    grad_spatial, grad_temporal = (
        lax.psum_scatter(
            tile_spatial.astype(jnp.bfloat16), "frame", scatter_dimension=1, tiled=True
        ).astype(jnp.float32),
        lax.psum_scatter(
            tile_temporal.astype(jnp.bfloat16), "frame", scatter_dimension=1, tiled=True
        ).astype(jnp.float32),
    )
    grad_scale = lax.rsqrt(position_count)
    return (
        grad_input,
        grad_scale * grad_spatial,
        grad_scale * grad_temporal,
        grad_scale * chan_gain,
        grad_scale * chan_shift,
    )


MESH = pl.DeviceIdType.MESH
BF = jnp.bfloat16
F32 = jnp.float32


def iota(shape, dim):
    return lax.broadcasted_iota(jnp.int32, shape, dim)


def row_of(column):
    n = column.shape[0]
    eye = iota((n, n), 0) == iota((n, n), 1)
    return jnp.sum(jnp.where(eye, column, 0.0), axis=0, keepdims=True)


def column_of(row):
    n = row.shape[1]
    eye = iota((n, n), 0) == iota((n, n), 1)
    return jnp.sum(jnp.where(eye, row, 0.0), axis=1, keepdims=True)


def group_column(row, size):
    n = row.shape[1]
    steps = 1 << 11
    factor = steps // size + 1
    same = (iota((n, n), 0) * factor) // steps == (iota((n, n), 1) * factor) // steps
    return jnp.sum(jnp.where(same, row, 0.0), axis=1, keepdims=True)


def blocked(rows, pad):
    n = rows.shape[1]
    parts = rows.reshape(8, -1, n)
    gap = jnp.zeros((8, pad - parts.shape[1], n), F32)
    return jnp.concatenate([parts, gap], axis=1).reshape(8 * pad, n)


def unblocked(rows, own):
    n = rows.shape[1]
    return rows.reshape(8, -1, n)[:, :own].reshape(8 * own, n)


def whole_kernel(
    lat, og, ws, wt, gain, shift, heights,
    gi, dws, dwt, dgain, dshift,
    g_s, g_t, p_s, p_t, r0s, r1s, r2s, r3s, r4s, r0t, r1t, r2t, r3t, r4t,
    ogf, sof, hsend, hrecv, ext, cols, zbuf, acc, normed_ref, pre_ref, gs_ref, gpre_ref,
    msg, tbuf, fbuf,
    ag_send, ag_recv, rs_send, rs_recv, fr_send, fr_recv, ha_send, ha_recv, st_send, st_recv,
):
    frames, tiles = 4, 8
    chans, cells = lat.shape
    own = ws.shape[0]
    pad = g_s.shape[3]
    sw, tw = ws.shape[1], wt.shape[1]
    group = chans // GROUPS
    f = lax.axis_index("frame")
    t = lax.axis_index("tile")
    y, x = f // 2, f % 2
    z, c = t // 2, t % 2
    zh, zl = z // 2, z % 2
    h = heights[0]
    live = iota((1, cells), 1) < h * COLUMNS
    short = h < STRIP_ROWS

    x_peer = (y * 2 + (1 - x), t)
    y_peer = ((1 - y) * 2 + x, t)
    z0_peer = (f, (zh * 2 + (1 - zl)) * 2 + c)
    z1_peer = (f, ((1 - zh) * 2 + zl) * 2 + c)
    c_peer = (f, z * 2 + (1 - c))

    barrier = pltpu.get_barrier_semaphore()
    for d in range(1, tiles):
        pl.semaphore_signal(barrier, inc=1, device_id=(f, (t + d) % tiles), device_id_type=MESH)
    for d in range(1, frames):
        pl.semaphore_signal(barrier, inc=1, device_id=((f + d) % frames, t), device_id_type=MESH)

    q_own = jnp.where(zh == 0, y, x)
    p_own = jnp.where(zh == 0, x, y)
    slot_own = q_own * 4 + p_own * 2 + zl
    for src, dst in ((ws, g_s), (wt, g_t)):
        wide = dst.shape[4]
        w32 = src[...].astype(F32)
        w32 = jnp.concatenate([w32, jnp.zeros((own, wide - w32.shape[1]), F32)], axis=1)
        w32 = jnp.concatenate([w32, jnp.zeros((pad - own, wide), F32)], axis=0)
        dst[c, zh, slot_own] = w32.astype(BF)
    pl.semaphore_wait(barrier, tiles + frames - 2)

    pending = []

    def remote(src, dst, ss, rs, peer):
        copy = pltpu.make_async_remote_copy(
            src_ref=src, dst_ref=dst, send_sem=ss, recv_sem=rs, device_id=peer, device_id_type=MESH
        )
        copy.start()
        pending.append(copy)
        return copy

    def gather_step(kind, step):
        buf = (g_t, g_s)[kind]
        if step == 0:
            moves = [(0, (c, zh, pl.ds(slot_own, 1)), z1_peer)]
        elif step == 1:
            moves = [
                (1, (c, 0, pl.ds(y * 4 + x * 2 + zl, 1)), z0_peer),
                (2, (c, 1, pl.ds(x * 4 + y * 2 + zl, 1)), z0_peer),
            ]
        elif step == 2:
            moves = [
                (3, (c, 0, pl.ds(y * 4 + x * 2, 2)), x_peer),
                (4, (c, 1, pl.ds(x * 4 + y * 2, 2)), y_peer),
            ]
        elif step == 3:
            moves = [
                (5, (c, 0, pl.ds(y * 4, 4)), y_peer),
                (6, (c, 1, pl.ds(x * 4, 4)), x_peer),
            ]
        else:
            moves = [(7, (c,), c_peer)]
        return [
            remote(buf.at[at], buf.at[at], ag_send.at[kind, i], ag_recv.at[kind, i], peer)
            for i, at, peer in moves
        ]

    def arrived(copies):
        for copy in copies:
            copy.wait_recv()

    def frame_copies(src, prev_dst, next_dst, base):
        up = pltpu.make_async_remote_copy(
            src_ref=src, dst_ref=prev_dst, send_sem=fr_send.at[base], recv_sem=fr_recv.at[base],
            device_id=((f + 1) % frames, t), device_id_type=MESH,
        )
        down = pltpu.make_async_remote_copy(
            src_ref=src, dst_ref=next_dst, send_sem=fr_send.at[base + 1], recv_sem=fr_recv.at[base + 1],
            device_id=((f + frames - 1) % frames, t), device_id_type=MESH,
        )
        return up, down

    def frame_start(pair):
        pl.when(f < frames - 1)(lambda: pair[0].start())
        pl.when(f > 0)(lambda: pair[1].start())

    def frame_arrived(pair):
        pl.when(f > 0)(lambda: pair[0].wait_recv())
        pl.when(f < frames - 1)(lambda: pair[1].wait_recv())

    def frame_sent(pair):
        pl.when(f < frames - 1)(lambda: pair[0].wait_send())
        pl.when(f > 0)(lambda: pair[1].wait_send())

    def strip_copies(which):
        down = pltpu.make_async_remote_copy(
            src_ref=hsend.at[which, 0], dst_ref=hrecv.at[which, 0],
            send_sem=ha_send.at[which, 0], recv_sem=ha_recv.at[which, 0],
            device_id=(f, (t + 1) % tiles), device_id_type=MESH,
        )
        up = pltpu.make_async_remote_copy(
            src_ref=hsend.at[which, 1], dst_ref=hrecv.at[which, 1],
            send_sem=ha_send.at[which, 1], recv_sem=ha_recv.at[which, 1],
            device_id=(f, (t + tiles - 1) % tiles), device_id_type=MESH,
        )
        return down, up

    def strip_start(pair, which, grid):
        half = cells // 2
        hsend[which, 0] = jnp.where(short, grid[:, :half], grid[:, half:]).astype(BF)
        hsend[which, 1] = grid[:, :half].astype(BF)
        pl.when(t < tiles - 1)(lambda: pair[0].start())
        pl.when(t > 0)(lambda: pair[1].start())

    def strip_arrived(pair):
        pl.when(t > 0)(lambda: pair[0].wait_recv())
        pl.when(t < tiles - 1)(lambda: pair[1].wait_recv())

    def strip_sent(pair):
        pl.when(t < tiles - 1)(lambda: pair[0].wait_send())
        pl.when(t > 0)(lambda: pair[1].wait_send())

    def strip_extended(which, grid):
        half = cells // 2
        above = hrecv[which, 0].astype(F32)
        below = hrecv[which, 1].astype(F32)
        return jnp.concatenate(
            [above, grid[:, :half], jnp.where(short, below, grid[:, half:]), below], axis=1
        )

    def sums_start(which, rows):
        width = msg.shape[2]
        for i, row in enumerate(rows):
            msg[which, 0, i : i + 1, 0:chans] = row
        tbuf[which, t] = msg[which, 0]
        return [
            remote(
                msg.at[which, 0], tbuf.at[which, t], st_send.at[which, d], st_recv.at[which, d],
                (f, (t + d) % tiles),
            )
            for d in range(1, tiles)
        ]

    def sums_middle(which, copies):
        arrived(copies)
        total = tbuf[which, 0]
        for i in range(1, tiles):
            total = total + tbuf[which, i]
        msg[which, 1] = total
        fbuf[which, f] = total
        return [
            remote(
                msg.at[which, 1], fbuf.at[which, f], st_send.at[which, tiles + d],
                st_recv.at[which, tiles + d], ((f + d) % frames, t),
            )
            for d in range(1, frames)
        ]

    def sums_end(which, copies):
        arrived(copies)
        total = fbuf[which, 0]
        for i in range(1, frames):
            total = total + fbuf[which, i]
        return total

    temporal = gather_step(0, 0)
    spatial = gather_step(1, 0)
    og_pair = frame_copies(og, ogf.at[0], ogf.at[1], 0)
    frame_start(og_pair)

    @pl.when(f == 0)
    def _():
        ogf[0] = jnp.zeros_like(ogf[0])
        sof[0:chans] = jnp.zeros((chans, cells), BF)

    @pl.when(f == frames - 1)
    def _():
        ogf[1] = jnp.zeros_like(ogf[1])
        sof[2 * chans : 3 * chans] = jnp.zeros((chans, cells), BF)

    @pl.when(t == 0)
    def _():
        hrecv[0, 0] = jnp.zeros_like(hrecv[0, 0])
        hrecv[1, 0] = jnp.zeros_like(hrecv[1, 0])

    @pl.when(t == tiles - 1)
    def _():
        hrecv[0, 1] = jnp.zeros_like(hrecv[0, 1])
        hrecv[1, 1] = jnp.zeros_like(hrecv[1, 1])

    sof[3 * chans :] = jnp.zeros((sof.shape[0] - 3 * chans, cells), BF)
    cols[9 * chans :] = jnp.zeros((cols.shape[0] - 9 * chans, cells), BF)
    msg[...] = jnp.zeros_like(msg)

    lat32 = lat[...].astype(F32)
    masked = jnp.where(live, lat32, 0.0)
    count_row = jnp.zeros((1, chans), F32) + h.astype(F32) * COLUMNS
    stat = sums_start(
        0,
        [
            row_of(jnp.sum(masked, axis=1, keepdims=True)),
            row_of(jnp.sum(masked * masked, axis=1, keepdims=True)),
            count_row,
        ],
    )
    arrived(temporal)
    temporal = gather_step(0, 1)
    stat = sums_middle(0, stat)
    arrived(spatial)
    spatial = gather_step(1, 1)
    arrived(temporal)
    temporal = gather_step(0, 2)
    total = sums_end(0, stat)
    count = total[2:3, 0:1]
    group_count = count * group
    gain_column = column_of(gain[...])
    shift_column = column_of(shift[...])
    mean = group_column(total[0:1, 0:chans], group) / group_count
    rstd = lax.rsqrt(
        group_column(total[1:2, 0:chans], group) / group_count - mean * mean + EPSILON
    )
    normed = (lat[...].astype(F32) - mean) * rstd
    pre = gain_column * normed + shift_column
    normed_ref[...] = normed
    pre_ref[...] = pre
    act = jnp.where(live, pre * jax.nn.sigmoid(pre), 0.0).astype(BF).astype(F32)
    act_pair = strip_copies(0)
    strip_start(act_pair, 0, act)
    arrived(temporal)
    temporal = gather_step(0, 3)
    arrived(spatial)
    spatial = gather_step(1, 2)
    frame_arrived(og_pair)
    arrived(temporal)
    temporal = gather_step(0, 4)
    strip_arrived(act_pair)
    ext[...] = strip_extended(0, act)

    width = ext.shape[1]
    chunk = 64
    col = iota((1, cells), 1) % COLUMNS
    left_ok = col >= 1
    right_ok = col < COLUMNS - 1
    half = cells // 2

    def cut(rolled, b):
        piece = rolled[:, half : half + cells]
        if b < 0:
            piece = jnp.where(left_ok, piece, 0.0)
        if b > 0:
            piece = jnp.where(right_ok, piece, 0.0)
        return piece

    def tap_rows(i, carry):
        r = pl.multiple_of(i * chunk, chunk)
        rows = ext[pl.ds(r, chunk)]
        for k in range(9):
            a, b = k // 3 - 1, k % 3 - 1
            s = a * COLUMNS + b
            rolled = pltpu.roll(rows, (-s) % width, 1) if s else rows
            cols[pl.ds(pl.multiple_of(k * chans + r, 64), chunk)] = cut(rolled, b).astype(BF)
        return carry

    lax.fori_loop(0, chans // chunk, tap_rows, 0)
    arrived(spatial)
    spatial = gather_step(1, 3)

    def weight(buf, fi):
        yi, xi = fi // 2, fi % 2
        blocks = []
        for ti in range(tiles):
            zi, ci = ti // 2, ti % 2
            hi, li = zi // 2, zi % 2
            qp = (yi * 4 + xi * 2) if hi == 0 else (xi * 4 + yi * 2)
            blocks.append(buf[ci, hi, qp + li])
        return jnp.concatenate(blocks, axis=0)

    def put(buf, fi, value):
        yi, xi = fi // 2, fi % 2
        for ti in range(tiles):
            zi, ci = ti // 2, ti % 2
            hi, li = zi // 2, zi % 2
            qp = (yi * 4 + xi * 2) if hi == 0 else (xi * 4 + yi * 2)
            buf[ci, hi, qp + li] = value[ti * pad : (ti + 1) * pad].astype(BF)

    contract_first = (((0,), (0,)), ((), ()))
    contract_last = (((1,), (1,)), ((), ()))

    arrived(temporal)
    og_here = blocked(jnp.where(live, og[...].astype(F32), 0.0), pad).astype(BF)
    og_next = blocked(jnp.where(live, ogf[1].astype(F32), 0.0), pad).astype(BF)
    og_prev = blocked(jnp.where(live, ogf[0].astype(F32), 0.0), pad).astype(BF)
    windows = (og_next, og_here, og_prev)
    for fi in range(frames):
        block = weight(g_t, fi)
        lo, hi = fi * tw, (fi + 1) * tw
        for k in range(3):
            first, last = max(lo, k * chans), min(hi, (k + 1) * chans)
            if first < last:
                part = lax.dot_general(
                    block, windows[k], contract_first, preferred_element_type=F32
                )
                zbuf[first:last, 0:cells] = part[first - lo : last - lo]
    gs = zbuf[0:chans, 0:cells] + zbuf[chans : 2 * chans, 0:cells]
    gs = gs + zbuf[2 * chans : 3 * chans, 0:cells]
    gs = jnp.where(live, gs, 0.0).astype(BF).astype(F32)
    gs_ref[...] = gs
    gs_pair = strip_copies(1)
    strip_start(gs_pair, 1, gs)

    def spatial_terms(fi, carry):
        here = blocked(gs_ref[...], pad).astype(BF)
        piece = cols[pl.ds(pl.multiple_of(fi * sw, 16), g_s.shape[4])]
        put(p_s, fi, lax.dot_general(here, piece, contract_last, preferred_element_type=F32))
        return carry

    lax.fori_loop(0, frames, spatial_terms, 0)

    def reduce_step(kind, step):
        buf = (p_t, p_s)[kind]
        into = ((r0t, r1t, r2t, r3t, r4t), (r0s, r1s, r2s, r3s, r4s))[kind][step]
        if step == 0:
            moves = [(0, (1 - c,), into, c_peer)]
        elif step == 1:
            moves = [
                (1, (c, 0, pl.ds((1 - y) * 4, 4)), into.at[0], y_peer),
                (2, (c, 1, pl.ds((1 - x) * 4, 4)), into.at[1], x_peer),
            ]
        elif step == 2:
            moves = [
                (3, (c, 0, pl.ds(y * 4 + (1 - x) * 2, 2)), into.at[0], x_peer),
                (4, (c, 1, pl.ds(x * 4 + (1 - y) * 2, 2)), into.at[1], y_peer),
            ]
        elif step == 3:
            moves = [
                (5, (c, 0, pl.ds(y * 4 + x * 2 + (1 - zl), 1)), into.at[0], z0_peer),
                (6, (c, 1, pl.ds(x * 4 + y * 2 + (1 - zl), 1)), into.at[1], z0_peer),
            ]
        else:
            q = jnp.where(zh == 0, x, y)
            p = jnp.where(zh == 0, y, x)
            moves = [(7, (c, 1 - zh, pl.ds(q * 4 + p * 2 + zl, 1)), into, z1_peer)]
        return [
            remote(buf.at[at], dst, rs_send.at[kind, i], rs_recv.at[kind, i], peer)
            for i, at, dst, peer in moves
        ]

    def reduce_add(kind, step):
        buf = (p_t, p_s)[kind]
        into = ((r0t, r1t, r2t, r3t), (r0s, r1s, r2s, r3s))[kind][step]
        blocks = (8, 4, 2, 1)[step]
        starts = (
            (0, 0),
            (y * 4, x * 4),
            (y * 4 + x * 2, x * 4 + y * 2),
            (y * 4 + x * 2 + zl, x * 4 + y * 2 + zl),
        )[step]
        for hi in range(2):
            def add(i, carry):
                here = buf[c, hi, starts[hi] + i].astype(F32) + into[hi, i].astype(F32)
                buf[c, hi, starts[hi] + i] = here.astype(BF)
                return carry

            lax.fori_loop(0, blocks, add, 0)

    rs_s = reduce_step(1, 0)
    arrived(spatial)
    spatial = gather_step(1, 4)
    strip_arrived(gs_pair)
    ext[...] = strip_extended(1, gs_ref[...])
    arrived(rs_s)
    reduce_add(1, 0)
    rs_s = reduce_step(1, 1)
    arrived(spatial)

    acc[...] = jnp.zeros_like(acc)

    def forward(fi, carry):
        piece = cols[pl.ds(pl.multiple_of(fi * sw, 16), g_s.shape[4])]
        acc[...] += jnp.dot(weight(g_s, fi), piece, preferred_element_type=F32)
        return carry

    lax.fori_loop(0, frames, forward, 0)
    spatial_out = jnp.where(live, unblocked(acc[...], own), 0.0).astype(BF)
    sof[chans : 2 * chans] = spatial_out
    so_pair = frame_copies(
        sof.at[pl.ds(chans, chans)], sof.at[pl.ds(0, chans)], sof.at[pl.ds(2 * chans, chans)], 2
    )
    frame_start(so_pair)

    gs_ext = blocked(ext[...], pad).astype(BF)
    for fi in range(frames):
        z_part = lax.dot_general(
            weight(g_s, fi), gs_ext, contract_first, preferred_element_type=F32
        )
        zbuf[fi * sw : (fi + 1) * sw] = z_part[0:sw]

    def tap_sum(i, carry):
        r = pl.multiple_of(i * chunk, chunk)
        total_rows = jnp.zeros((chunk, cells), F32)
        for k in range(9):
            a, b = k // 3 - 1, k % 3 - 1
            s = a * COLUMNS + b
            rows = zbuf[pl.ds(pl.multiple_of(k * chans + r, 64), chunk)]
            rolled = pltpu.roll(rows, s % width, 1) if s else rows
            total_rows = total_rows + cut(rolled, -b)
        pre_rows = pre_ref[pl.ds(r, chunk)]
        sig = jax.nn.sigmoid(pre_rows)
        gpre_ref[pl.ds(r, chunk)] = jnp.where(
            live, total_rows * sig * (1.0 + pre_rows * (1.0 - sig)), 0.0
        )
        return carry

    lax.fori_loop(0, chans // chunk, tap_sum, 0)
    stat = sums_start(
        1,
        [
            row_of(jnp.sum(gpre_ref[...] * normed_ref[...], axis=1, keepdims=True)),
            row_of(jnp.sum(gpre_ref[...], axis=1, keepdims=True)),
        ],
    )

    frame_arrived(so_pair)
    for fi in range(frames):
        piece = sof[fi * tw : fi * tw + g_t.shape[4]]
        put(p_t, fi, lax.dot_general(og_here, piece, contract_last, preferred_element_type=F32))
    rs_t = reduce_step(0, 0)
    stat = sums_middle(1, stat)
    arrived(rs_s)
    reduce_add(1, 1)
    rs_s = reduce_step(1, 2)
    arrived(rs_t)
    reduce_add(0, 0)
    rs_t = reduce_step(0, 1)
    sums = sums_end(1, stat)
    arrived(rs_s)
    reduce_add(1, 2)
    rs_s = reduce_step(1, 3)
    arrived(rs_t)
    reduce_add(0, 1)
    rs_t = reduce_step(0, 2)

    scale = lax.rsqrt(count)
    chan_gain, chan_shift = sums[0:1, 0:chans], sums[1:2, 0:chans]
    dgain[...] = scale * chan_gain
    dshift[...] = scale * chan_shift
    shift_sum = group_column(gain[...] * chan_shift, group) / group_count
    gain_sum = group_column(gain[...] * chan_gain, group) / group_count
    result = og[...].astype(F32) + rstd * (
        gain_column * gpre_ref[...] - shift_sum - normed_ref[...] * gain_sum
    )
    gi[...] = jnp.where(live, result, 0.0).astype(BF)

    arrived(rs_s)
    reduce_add(1, 3)
    rs_s = reduce_step(1, 4)
    arrived(rs_t)
    reduce_add(0, 2)
    rs_t = reduce_step(0, 3)
    arrived(rs_t)
    reduce_add(0, 3)
    rs_t = reduce_step(0, 4)
    arrived(rs_s)
    dws[...] = scale * (p_s[c, zh, slot_own].astype(F32) + r4s[0].astype(F32))[0:own, 0:sw]
    arrived(rs_t)
    dwt[...] = scale * (p_t[c, zh, slot_own].astype(F32) + r4t[0].astype(F32))[0:own, 0:tw]

    for copy in pending:
        copy.wait_send()
    for pair in (og_pair, so_pair):
        frame_sent(pair)
    for pair in (act_pair, gs_pair):
        strip_sent(pair)


def fused(latents, out_grad, w_spatial, w_temporal, norm_gain, norm_shift, heights):
    chans, cells = latents.shape[1:]
    own, sw = w_spatial.shape
    tw = w_temporal.shape[1]
    pad = -(-own // 16) * 16
    sp, tp = -(-sw // 128) * 128, -(-tw // 128) * 128
    wide = -(-chans // 128) * 128

    def blocks(lead, kind):
        return pltpu.VMEM(lead + (pad, kind), BF)

    scratch = (
        [blocks((2, 2, 8), sp), blocks((2, 2, 8), tp), blocks((2, 2, 8), sp), blocks((2, 2, 8), tp)]
        + [
            blocks(lead, kind)
            for kind in (sp, tp)
            for lead in ((2, 8), (2, 4), (2, 2), (2, 1), (1,))
        ]
        + [
            pltpu.VMEM((2, chans, cells), BF),
            pltpu.VMEM((3 * chans + tp - tw, cells), BF),
            pltpu.VMEM((2, 2, chans, cells // 2), BF),
            pltpu.VMEM((2, 2, chans, cells // 2), BF),
            pltpu.VMEM((chans, 2 * cells), F32),
            pltpu.VMEM((9 * chans + sp - sw, cells), BF),
            pltpu.VMEM((9 * chans, 2 * cells), F32),
            pltpu.VMEM((8 * pad, cells), F32),
        ]
        + [pltpu.VMEM((chans, cells), F32)] * 4
        + [
            pltpu.VMEM((2, 2, 8, wide), F32),
            pltpu.VMEM((2, 8, 8, wide), F32),
            pltpu.VMEM((2, 4, 8, wide), F32),
        ]
        + [pltpu.SemaphoreType.DMA((2, 8))] * 4
        + [pltpu.SemaphoreType.DMA((4,))] * 2
        + [pltpu.SemaphoreType.DMA((2, 2))] * 2
        + [pltpu.SemaphoreType.DMA((2, 12))] * 2
    )
    vmem = pl.BlockSpec(memory_space=pltpu.VMEM)
    outs = pl.pallas_call(
        whole_kernel,
        out_shape=(
            jax.ShapeDtypeStruct((chans, cells), BF),
            jax.ShapeDtypeStruct((own, sw), F32),
            jax.ShapeDtypeStruct((own, tw), F32),
            jax.ShapeDtypeStruct((1, chans), F32),
            jax.ShapeDtypeStruct((1, chans), F32),
        ),
        in_specs=[vmem] * 6 + [pl.BlockSpec(memory_space=pltpu.SMEM)],
        out_specs=(vmem,) * 5,
        scratch_shapes=scratch,
        compiler_params=pltpu.CompilerParams(
            collective_id=0, has_side_effects=True, vmem_limit_bytes=56 * 1024 * 1024
        ),
    )(
        latents[0], out_grad[0], w_spatial, w_temporal, norm_gain[None], norm_shift[None], heights
    )
    return outs[0][None], outs[1], outs[2], outs[3][0], outs[4][0]


def solution(mesh):
    in_specs = (
        P("frame", None, "tile"),
        P("frame", None, "tile"),
        P("tile", "frame"),
        P("tile", "frame"),
        P(),
        P(),
        P("tile"),
    )
    out_specs = (P("frame", None, "tile"), P("tile", "frame"), P("tile", "frame"), P(), P())
    fits = mesh.shape["frame"] == 4 and mesh.shape["tile"] == 8
    return jax.shard_map(
        fused if fits else local, mesh=mesh, in_specs=in_specs, out_specs=out_specs, check_vma=False
    )
```

```python
import jax
import jax.numpy as jnp
from jax import lax
from jax.experimental import pallas as pl
from jax.experimental.pallas import tpu as pltpu
from jax.sharding import PartitionSpec as P

GROUPS = 32
COLUMNS = 16
STRIP_ROWS = 16


EPSILON = 1e-05


def from_behind(shard, axis, by):
    peers = lax.axis_size(axis)
    pairs = [(i, i + by) for i in range(peers) if 0 <= i + by < peers]
    return lax.ppermute(shard, axis, pairs)


def padded_2(cells, sides, width):
    for axis, dim in sides:
        count = lax.axis_size(axis)
        ends = count - 1
        head = lax.slice_in_dim(cells, 0, width, axis=dim)
        tail = lax.slice_in_dim(cells, cells.shape[dim] - width, cells.shape[dim], axis=dim)
        cells = jnp.concatenate(
            [
                lax.ppermute(tail, axis, [(i, (i + 1) % count) for i in range(ends)]),
                cells,
                lax.ppermute(head, axis, [((i + 1) % count, i) for i in range(ends)]),
            ],
            axis=dim,
        )
    return cells


def flip_taps(weight, tap_count):
    outputs = weight.shape[0]
    return jnp.transpose(weight.reshape(outputs, tap_count, -1)[:, ::-1, :], (2, 1, 0)).reshape(
        -1, tap_count * outputs
    )


def padded_rows(row_grid, above_row, below_row, height):
    channel_count = row_grid.shape[0]
    padded = jnp.zeros((channel_count, STRIP_ROWS + 2, COLUMNS + 2), row_grid.dtype)
    padded = padded.at[:, 1 : STRIP_ROWS + 1, 1 : COLUMNS + 1].set(row_grid)
    padded = padded.at[:, 0, 1 : COLUMNS + 1].set(above_row)
    below_block = jnp.pad(below_row, ((0, 0), (1, 1)))[:, None, :]
    return lax.dynamic_update_slice(padded, below_block, (jnp.int32(0), height + 1, jnp.int32(0)))


def tap_columns(padded, row_count):
    pieces = [
        padded[:, row_step : row_step + row_count, col_step : col_step + COLUMNS]
        for row_step in range(3)
        for col_step in range(3)
    ]
    return jnp.stack(pieces, axis=0).reshape(9 * padded.shape[0], row_count * COLUMNS)


def local(latents, out_grad, w_spatial, w_temporal, norm_gain, norm_shift, heights):
    channel_count = latents.shape[1]
    cell_count = latents.shape[2]
    group_size = channel_count // GROUPS
    height = heights[0]
    slot_row = jnp.arange(cell_count, dtype=jnp.int32) // COLUMNS
    live_cells = slot_row < height
    live_float = live_cells.astype(jnp.float32)
    contract_last = (((1,), (1,)), ((), ()))
    part_spatial_w, part_temporal_w = (
        lax.all_gather(w_spatial, "frame", axis=1, tiled=True),
        lax.all_gather(w_temporal, "frame", axis=1, tiled=True),
    )
    spatial_full, temporal_full = (
        lax.all_gather(part_spatial_w, "tile", axis=0, tiled=True),
        lax.all_gather(part_temporal_w, "tile", axis=0, tiled=True),
    )
    latent_full = latents[0].astype(jnp.float32)
    masked = latent_full * live_float[None, :]
    group_sum = masked.reshape(GROUPS, group_size, cell_count).sum(axis=(1, 2))
    group_square = (masked * latent_full).reshape(GROUPS, group_size, cell_count).sum(axis=(1, 2))
    own_count = height.astype(jnp.float32) * COLUMNS
    total_sum, total_square, position_count = lax.psum(
        (group_sum, group_square, own_count), ("frame", "tile")
    )
    group_count = position_count * group_size
    group_mean = total_sum / group_count
    group_rstd = lax.rsqrt(total_square / group_count - group_mean * group_mean + EPSILON)
    mean_column = jnp.repeat(group_mean, group_size)[:, None]
    rstd_column = jnp.repeat(group_rstd, group_size)[:, None]
    gain_column = norm_gain[:, None]
    normed = (latent_full - mean_column) * rstd_column
    pre_act = gain_column * normed + norm_shift[:, None]
    activated = jnp.where(live_cells[None, :], jax.nn.silu(pre_act), 0.0).astype(jnp.bfloat16)
    act_grid = activated.reshape(channel_count, STRIP_ROWS, COLUMNS)
    last_live = lax.dynamic_slice_in_dim(act_grid, height - 1, 1, 1)[:, 0, :]
    from_above = from_behind(last_live, "tile", 1)
    from_below = from_behind(act_grid[:, 0, :], "tile", -1)
    act_padded = padded_rows(act_grid, from_above, from_below, height)
    act_columns = tap_columns(act_padded, STRIP_ROWS)
    spatial_raw = jnp.dot(spatial_full, act_columns, preferred_element_type=jnp.float32)
    spatial_out = jnp.where(live_cells[None, :], spatial_raw, 0.0).astype(jnp.bfloat16)
    spatial_frames = padded_2(spatial_out[None], (("frame", 0),), 1)
    grad_here = jnp.where(live_cells[None, :], out_grad[0], jnp.zeros((), jnp.bfloat16))
    grad_frames = padded_2(grad_here[None], (("frame", 0),), 1)
    part_temporal = lax.dot_general(
        grad_here,
        spatial_frames.reshape(3 * channel_count, cell_count),
        contract_last,
        preferred_element_type=jnp.float32,
    )
    grad_spat = jnp.dot(
        flip_taps(temporal_full, 3),
        grad_frames.reshape(3 * channel_count, cell_count),
        preferred_element_type=jnp.float32,
    )
    grad_spat = jnp.where(live_cells[None, :], grad_spat, 0.0).astype(jnp.bfloat16)
    spat_grid = grad_spat.reshape(channel_count, STRIP_ROWS, COLUMNS)
    grad_last = lax.dynamic_slice_in_dim(spat_grid, height - 1, 1, 1)[:, 0, :]
    grad_above = from_behind(grad_last, "tile", 1)
    grad_below = from_behind(spat_grid[:, 0, :], "tile", -1)
    grad_padded = padded_rows(spat_grid, grad_above, grad_below, height)
    spatial_flip = flip_taps(spatial_full, 9)
    grad_act = jnp.dot(
        spatial_flip, tap_columns(grad_padded, STRIP_ROWS), preferred_element_type=jnp.float32
    )
    part_spatial = lax.dot_general(
        grad_spat, act_columns, contract_last, preferred_element_type=jnp.float32
    )
    sigmoid_act = jax.nn.sigmoid(pre_act)
    grad_pre = jnp.where(
        live_cells[None, :], grad_act * sigmoid_act * (1.0 + pre_act * (1.0 - sigmoid_act)), 0.0
    )
    chan_gain, chan_shift = lax.psum(
        (jnp.sum(grad_pre * normed, axis=1), jnp.sum(grad_pre, axis=1)), ("frame", "tile")
    )
    shift_sum = (norm_gain * chan_shift).reshape(GROUPS, group_size).sum(1) / group_count
    gain_sum = (norm_gain * chan_gain).reshape(GROUPS, group_size).sum(1) / group_count
    result = grad_here.astype(jnp.float32) + rstd_column * (
        gain_column * grad_pre
        - jnp.repeat(shift_sum, group_size)[:, None]
        - normed * jnp.repeat(gain_sum, group_size)[:, None]
    )
    grad_input = jnp.where(live_cells[None, :], result, 0.0).astype(jnp.bfloat16)[None]
    tile_spatial, tile_temporal = (
        lax.psum_scatter(
            part_spatial.astype(jnp.bfloat16), "tile", scatter_dimension=0, tiled=True
        ).astype(jnp.float32),
        lax.psum_scatter(
            part_temporal.astype(jnp.bfloat16), "tile", scatter_dimension=0, tiled=True
        ).astype(jnp.float32),
    )
    grad_spatial, grad_temporal = (
        lax.psum_scatter(
            tile_spatial.astype(jnp.bfloat16), "frame", scatter_dimension=1, tiled=True
        ).astype(jnp.float32),
        lax.psum_scatter(
            tile_temporal.astype(jnp.bfloat16), "frame", scatter_dimension=1, tiled=True
        ).astype(jnp.float32),
    )
    grad_scale = lax.rsqrt(position_count)
    return (
        grad_input,
        grad_scale * grad_spatial,
        grad_scale * grad_temporal,
        grad_scale * chan_gain,
        grad_scale * chan_shift,
    )


MESH = pl.DeviceIdType.MESH
BF = jnp.bfloat16
F32 = jnp.float32


def iota(shape, dim):
    return lax.broadcasted_iota(jnp.int32, shape, dim)


def row_of(column):
    n = column.shape[0]
    eye = iota((n, n), 0) == iota((n, n), 1)
    return jnp.sum(jnp.where(eye, column, 0.0), axis=0, keepdims=True)


def column_of(row):
    n = row.shape[1]
    eye = iota((n, n), 0) == iota((n, n), 1)
    return jnp.sum(jnp.where(eye, row, 0.0), axis=1, keepdims=True)


def group_column(row, size):
    n = row.shape[1]
    steps = 1 << 11
    factor = steps // size + 1
    same = (iota((n, n), 0) * factor) // steps == (iota((n, n), 1) * factor) // steps
    return jnp.sum(jnp.where(same, row, 0.0), axis=1, keepdims=True)


def whole_kernel(
    lat, og, ws, wt, gain, shift, heights,
    gi, dws, dwt, dgain, dshift,
    g_t, g_a, g_b, p_t, p_a, p_b,
    r0t, r0a, r0b, r1t, r1a, r1b, r2t, r2a, r2b, r3t, r3a, r3b, r4t, r4a, r4b,
    xs_t, xs_a, xs_b, xr_t, xr_a, xr_b, ys_t, ys_a, ys_b, yr_t, yr_a, yr_b,
    ogf, sof, hsend, hrecv, ext, cols, zbuf, acc, normed_ref, pre_ref, gs_ref, gpre_ref,
    msg, tbuf, fbuf,
    ag_send, ag_recv, rs_send, rs_recv, fr_send, fr_recv, ha_send, ha_recv, st_send, st_recv, tr_send, tr_recv,
):
    frames, tiles = 4, 8
    chans, cells = lat.shape
    own = ws.shape[0]
    lanes = tuple(buf.shape[4] for buf in (g_t, g_a, g_b))
    rows_in = 2 * own
    sp = 2 * (lanes[1] + lanes[2])
    tp = 2 * lanes[0]
    gathered, partial = (g_t, g_a, g_b), (p_t, p_a, p_b)
    landing = (
        (r0t, r0a, r0b), (r1t, r1a, r1b), (r2t, r2a, r2b), (r3t, r3a, r3b), (r4t, r4a, r4b),
    )
    sw, tw = ws.shape[1], wt.shape[1]
    group = chans // GROUPS
    f = lax.axis_index("frame")
    t = lax.axis_index("tile")
    y, x = f // 2, f % 2
    z, c = t // 2, t % 2
    zh, zl = z // 2, z % 2
    h = heights[0]
    live = iota((1, cells), 1) < h * COLUMNS
    short = h < STRIP_ROWS

    x_peer = (y * 2 + (1 - x), t)
    y_peer = ((1 - y) * 2 + x, t)
    z0_peer = (f, (zh * 2 + (1 - zl)) * 2 + c)
    z1_peer = (f, ((1 - zh) * 2 + zl) * 2 + c)
    c_peer = (f, z * 2 + (1 - c))

    barrier = pltpu.get_barrier_semaphore()
    for d in range(1, tiles):
        pl.semaphore_signal(barrier, inc=1, device_id=(f, (t + d) % tiles), device_id_type=MESH)
    for d in range(1, frames):
        pl.semaphore_signal(barrier, inc=1, device_id=((f + d) % frames, t), device_id_type=MESH)

    q_own = jnp.where(zh == 0, y, x)
    p_own = jnp.where(zh == 0, x, y)
    slot_own = q_own * 4 + p_own * 2 + zl
    def halves(src, wide):
        w32 = src[...].astype(F32)
        w32 = jnp.concatenate([w32, jnp.zeros((own, wide - w32.shape[1]), F32)], axis=1)
        first, second = w32[:, : wide // 2], w32[:, wide // 2 :]
        return jnp.where(c == 0, first, second), jnp.where(c == 0, second, first)

    kept_t, sent_t = halves(wt, tp)
    kept_s, sent_s = halves(ws, sp)
    kept = (kept_t, kept_s[:, : lanes[1]], kept_s[:, lanes[1] :])
    sent = (sent_t, sent_s[:, : lanes[1]], sent_s[:, lanes[1] :])

    def staged(ref, rows):
        ref[...] = jnp.concatenate(
            [rows, jnp.zeros((ref.shape[0] - own, rows.shape[1]), F32)], axis=0
        ).astype(BF)

    for ref, rows in zip((xs_t, xs_a, xs_b), sent):
        staged(ref, rows)
    pl.semaphore_wait(barrier, tiles + frames - 2)

    pending = []

    def remote(src, dst, ss, rs, peer):
        copy = pltpu.make_async_remote_copy(
            src_ref=src, dst_ref=dst, send_sem=ss, recv_sem=rs, device_id=peer, device_id_type=MESH
        )
        copy.start()
        pending.append(copy)
        return copy

    def trade(which, kind, src, dst):
        return [
            remote(src, dst, tr_send.at[which, kind], tr_recv.at[which, kind], c_peer)
        ]

    def gather_step(kind, step):
        buf = gathered[kind]
        if step == 0:
            moves = [(0, (c, zh, pl.ds(slot_own, 1)), z1_peer)]
        elif step == 1:
            moves = [
                (1, (c, 0, pl.ds(y * 4 + x * 2 + zl, 1)), z0_peer),
                (2, (c, 1, pl.ds(x * 4 + y * 2 + zl, 1)), z0_peer),
            ]
        elif step == 2:
            moves = [
                (3, (c, 0, pl.ds(y * 4 + x * 2, 2)), x_peer),
                (4, (c, 1, pl.ds(x * 4 + y * 2, 2)), y_peer),
            ]
        elif step == 3:
            moves = [
                (5, (c, 0, pl.ds(y * 4, 4)), y_peer),
                (6, (c, 1, pl.ds(x * 4, 4)), x_peer),
            ]
        else:
            moves = [(7, (c,), c_peer)]
        return [
            remote(buf.at[at], buf.at[at], ag_send.at[kind, i], ag_recv.at[kind, i], peer)
            for i, at, peer in moves
        ]

    def arrived(copies):
        for copy in copies:
            copy.wait_recv()

    def frame_copies(src, prev_dst, next_dst, base):
        up = pltpu.make_async_remote_copy(
            src_ref=src, dst_ref=prev_dst, send_sem=fr_send.at[base], recv_sem=fr_recv.at[base],
            device_id=((f + 1) % frames, t), device_id_type=MESH,
        )
        down = pltpu.make_async_remote_copy(
            src_ref=src, dst_ref=next_dst, send_sem=fr_send.at[base + 1], recv_sem=fr_recv.at[base + 1],
            device_id=((f + frames - 1) % frames, t), device_id_type=MESH,
        )
        return up, down

    def frame_start(pair):
        pl.when(f < frames - 1)(lambda: pair[0].start())
        pl.when(f > 0)(lambda: pair[1].start())

    def frame_arrived(pair):
        pl.when(f > 0)(lambda: pair[0].wait_recv())
        pl.when(f < frames - 1)(lambda: pair[1].wait_recv())

    def frame_sent(pair):
        pl.when(f < frames - 1)(lambda: pair[0].wait_send())
        pl.when(f > 0)(lambda: pair[1].wait_send())

    def strip_copies(which):
        down = pltpu.make_async_remote_copy(
            src_ref=hsend.at[which, 0], dst_ref=hrecv.at[which, 0],
            send_sem=ha_send.at[which, 0], recv_sem=ha_recv.at[which, 0],
            device_id=(f, (t + 1) % tiles), device_id_type=MESH,
        )
        up = pltpu.make_async_remote_copy(
            src_ref=hsend.at[which, 1], dst_ref=hrecv.at[which, 1],
            send_sem=ha_send.at[which, 1], recv_sem=ha_recv.at[which, 1],
            device_id=(f, (t + tiles - 1) % tiles), device_id_type=MESH,
        )
        return down, up

    def strip_start(pair, which, grid):
        half = cells // 2
        hsend[which, 0] = jnp.where(short, grid[:, :half], grid[:, half:]).astype(BF)
        hsend[which, 1] = grid[:, :half].astype(BF)
        pl.when(t < tiles - 1)(lambda: pair[0].start())
        pl.when(t > 0)(lambda: pair[1].start())

    def strip_arrived(pair):
        pl.when(t > 0)(lambda: pair[0].wait_recv())
        pl.when(t < tiles - 1)(lambda: pair[1].wait_recv())

    def strip_sent(pair):
        pl.when(t < tiles - 1)(lambda: pair[0].wait_send())
        pl.when(t > 0)(lambda: pair[1].wait_send())

    def strip_extended(which, grid):
        half = cells // 2
        above = hrecv[which, 0].astype(F32)
        below = hrecv[which, 1].astype(F32)
        return jnp.concatenate(
            [above, grid[:, :half], jnp.where(short, below, grid[:, half:]), below], axis=1
        )

    stride = msg.shape[3] // 3

    def sums_start(which, rows):
        row = jnp.zeros((1, msg.shape[3]), F32)
        for i, part in enumerate(rows):
            at = i * stride
            row_parts = [jnp.zeros((1, at), F32)] if at else []
            row_parts.append(part)
            rest = msg.shape[3] - at - part.shape[1]
            if rest:
                row_parts.append(jnp.zeros((1, rest), F32))
            row = row + jnp.concatenate(row_parts, axis=1)
        msg[which, 0] = row
        tbuf[which, t] = msg[which, 0]
        return [
            remote(
                msg.at[which, 0], tbuf.at[which, t], st_send.at[which, d], st_recv.at[which, d],
                (f, (t + d) % tiles),
            )
            for d in range(1, tiles)
        ]

    def sums_middle(which, copies):
        arrived(copies)
        total = tbuf[which, 0]
        for i in range(1, tiles):
            total = total + tbuf[which, i]
        msg[which, 1] = total
        fbuf[which, f] = total
        return [
            remote(
                msg.at[which, 1], fbuf.at[which, f], st_send.at[which, tiles + d],
                st_recv.at[which, tiles + d], ((f + d) % frames, t),
            )
            for d in range(1, frames)
        ]

    def sums_end(which, copies):
        arrived(copies)
        total = fbuf[which, 0]
        for i in range(1, frames):
            total = total + fbuf[which, i]
        return total

    traded = [
        trade(0, kind, src, dst)
        for kind, (src, dst) in enumerate(((xs_t, xr_t), (xs_a, xr_a), (xs_b, xr_b)))
    ]
    og_pair = frame_copies(og, ogf.at[0], ogf.at[1], 0)
    frame_start(og_pair)

    @pl.when(f == 0)
    def _():
        ogf[0] = jnp.zeros_like(ogf[0])
        sof[0:chans] = jnp.zeros((chans, cells), BF)

    @pl.when(f == frames - 1)
    def _():
        ogf[1] = jnp.zeros_like(ogf[1])
        sof[2 * chans : 3 * chans] = jnp.zeros((chans, cells), BF)

    @pl.when(t == 0)
    def _():
        hrecv[0, 0] = jnp.zeros_like(hrecv[0, 0])
        hrecv[1, 0] = jnp.zeros_like(hrecv[1, 0])

    @pl.when(t == tiles - 1)
    def _():
        hrecv[0, 1] = jnp.zeros_like(hrecv[0, 1])
        hrecv[1, 1] = jnp.zeros_like(hrecv[1, 1])

    sof[3 * chans :] = jnp.zeros((sof.shape[0] - 3 * chans, cells), BF)
    cols[9 * chans :] = jnp.zeros((cols.shape[0] - 9 * chans, cells), BF)

    lat32 = lat[...].astype(F32)
    masked = jnp.where(live, lat32, 0.0)
    count_row = jnp.zeros((1, 128), F32) + h.astype(F32) * COLUMNS
    stat = sums_start(
        0,
        [
            row_of(jnp.sum(masked, axis=1, keepdims=True)),
            row_of(jnp.sum(masked * masked, axis=1, keepdims=True)),
            count_row,
        ],
    )
    chain = [None] * 3
    for kind, ref in enumerate((xr_t, xr_a, xr_b)):
        arrived(traded[kind])
        other = ref[0:own].astype(F32)
        gathered[kind][c, zh, slot_own] = jnp.concatenate(
            [jnp.where(c == 0, kept[kind], other), jnp.where(c == 0, other, kept[kind])], axis=0
        ).astype(BF)
        chain[kind] = gather_step(kind, 0)

    def forth(kind, step):
        arrived(chain[kind])
        if step < 5:
            chain[kind] = gather_step(kind, step)

    forth(0, 1)
    stat = sums_middle(0, stat)
    forth(1, 1)
    forth(2, 1)
    forth(0, 2)
    total = sums_end(0, stat)
    count = total[:, 2 * stride : 2 * stride + 1]
    group_count = count * group
    gain_row = gain[...].reshape(1, chans)
    gain_column = column_of(gain_row)
    shift_column = column_of(shift[...].reshape(1, chans))
    mean = group_column(total[:, 0:chans], group) / group_count
    rstd = lax.rsqrt(
        group_column(total[:, stride : stride + chans], group) / group_count - mean * mean + EPSILON
    )
    normed = (lat[...].astype(F32) - mean) * rstd
    pre = gain_column * normed + shift_column
    normed_ref[...] = normed
    pre_ref[...] = pre
    act = jnp.where(live, pre * jax.nn.sigmoid(pre), 0.0).astype(BF).astype(F32)
    act_pair = strip_copies(0)
    strip_start(act_pair, 0, act)
    forth(1, 2)
    forth(0, 3)
    forth(2, 2)
    frame_arrived(og_pair)
    og_here = jnp.where(live, og[...], jnp.zeros((), BF))
    og_next = jnp.where(live, ogf[1], jnp.zeros((), BF))
    og_prev = jnp.where(live, ogf[0], jnp.zeros((), BF))
    forth(1, 3)
    forth(0, 4)
    forth(2, 3)
    strip_arrived(act_pair)
    ext[...] = strip_extended(0, act)

    width = ext.shape[1]
    chunk = 64
    col = iota((1, cells), 1) % COLUMNS
    left_ok = col >= 1
    right_ok = col < COLUMNS - 1
    half = cells // 2

    def cut(rolled, b):
        piece = rolled[:, half : half + cells]
        if b < 0:
            piece = jnp.where(left_ok, piece, 0.0)
        if b > 0:
            piece = jnp.where(right_ok, piece, 0.0)
        return piece

    def tap_rows(i, carry):
        r = pl.multiple_of(i * chunk, chunk)
        rows = ext[pl.ds(r, chunk)]
        for k in range(9):
            a, b = k // 3 - 1, k % 3 - 1
            s = a * COLUMNS + b
            rolled = pltpu.roll(rows, (-s) % width, 1) if s else rows
            cols[pl.ds(pl.multiple_of(k * chans + r, 64), chunk)] = cut(rolled, b).astype(BF)
        return carry

    lax.fori_loop(0, chans // chunk, tap_rows, 0)

    def slots(fi):
        yi, xi = fi // 2, fi % 2
        return yi * 4 + xi * 2, xi * 4 + yi * 2

    def weight(bufs, fi):
        at = slots(fi)
        sides = []
        for side in range(2):
            for buf in bufs:
                sides.append(
                    jnp.concatenate(
                        [buf[side, zi // 2, at[zi // 2] + zi % 2] for zi in range(4)], axis=0
                    )
                )
        return jnp.concatenate(sides, axis=1)

    def put(bufs, fi, value):
        at = slots(fi)
        lane = 0
        for side in range(2):
            for buf in bufs:
                wide = buf.shape[4]
                for zi in range(4):
                    buf[side, zi // 2, at[zi // 2] + zi % 2] = value[
                        zi * rows_in : (zi + 1) * rows_in, lane : lane + wide
                    ].astype(BF)
                lane += wide

    contract_first = (((0,), (0,)), ((), ()))
    contract_last = (((1,), (1,)), ((), ()))

    forth(0, 5)
    windows = (og_next, og_here, og_prev)
    for fi in range(frames):
        block = weight((g_t,), fi)
        lo, hi = fi * tw, (fi + 1) * tw
        for k in range(3):
            first, last = max(lo, k * chans), min(hi, (k + 1) * chans)
            if first < last:
                part = lax.dot_general(
                    block, windows[k], contract_first, preferred_element_type=F32
                )
                zbuf[first:last, 0:cells] = part[first - lo : last - lo]
    gs = zbuf[0:chans, 0:cells] + zbuf[chans : 2 * chans, 0:cells]
    gs = gs + zbuf[2 * chans : 3 * chans, 0:cells]
    gs = jnp.where(live, gs, 0.0).astype(BF).astype(F32)
    gs_ref[...] = gs
    gs_pair = strip_copies(1)
    strip_start(gs_pair, 1, gs)

    def spatial_terms(fi, carry):
        here = gs_ref[...].astype(BF)
        piece = cols[pl.ds(pl.multiple_of(fi * sw, 16), sp)]
        put((p_a, p_b), fi, lax.dot_general(here, piece, contract_last, preferred_element_type=F32))
        return carry

    lax.fori_loop(0, frames, spatial_terms, 0)

    def reduce_step(kind, step):
        buf = partial[kind]
        into = landing[step][kind]
        if step == 0:
            moves = [(0, (1 - c,), into, c_peer)]
        elif step == 1:
            moves = [
                (1, (c, 0, pl.ds((1 - y) * 4, 4)), into.at[0], y_peer),
                (2, (c, 1, pl.ds((1 - x) * 4, 4)), into.at[1], x_peer),
            ]
        elif step == 2:
            moves = [
                (3, (c, 0, pl.ds(y * 4 + (1 - x) * 2, 2)), into.at[0], x_peer),
                (4, (c, 1, pl.ds(x * 4 + (1 - y) * 2, 2)), into.at[1], y_peer),
            ]
        elif step == 3:
            moves = [
                (5, (c, 0, pl.ds(y * 4 + x * 2 + (1 - zl), 1)), into.at[0], z0_peer),
                (6, (c, 1, pl.ds(x * 4 + y * 2 + (1 - zl), 1)), into.at[1], z0_peer),
            ]
        else:
            q = jnp.where(zh == 0, x, y)
            p = jnp.where(zh == 0, y, x)
            moves = [(7, (c, 1 - zh, pl.ds(q * 4 + p * 2 + zl, 1)), into, z1_peer)]
        return [
            remote(buf.at[at], dst, rs_send.at[kind, i], rs_recv.at[kind, i], peer)
            for i, at, dst, peer in moves
        ]

    def reduce_add(kind, step):
        buf = partial[kind]
        into = landing[step][kind]
        blocks = (8, 4, 2, 1)[step]
        starts = (
            (0, 0),
            (y * 4, x * 4),
            (y * 4 + x * 2, x * 4 + y * 2),
            (y * 4 + x * 2 + zl, x * 4 + y * 2 + zl),
        )[step]
        for hi in range(2):
            def add(i, carry):
                here = buf[c, hi, starts[hi] + i].astype(F32) + into[hi, i].astype(F32)
                buf[c, hi, starts[hi] + i] = here.astype(BF)
                return carry

            lax.fori_loop(0, blocks, add, 0)

    back = [None] * 3

    def reduce_start(kind):
        back[kind] = reduce_step(kind, 0)

    def reduce_on(kind, step):
        arrived(back[kind])
        reduce_add(kind, step - 1)
        back[kind] = reduce_step(kind, step)

    forth(1, 4)
    forth(2, 4)
    reduce_start(1)
    reduce_start(2)
    strip_arrived(gs_pair)
    ext[...] = strip_extended(1, gs_ref[...])
    forth(1, 5)
    forth(2, 5)
    reduce_on(1, 1)

    acc[...] = jnp.zeros_like(acc)

    def forward(fi, carry):
        piece = cols[pl.ds(pl.multiple_of(fi * sw, 16), sp)]
        acc[...] += jnp.dot(weight((g_a, g_b), fi), piece, preferred_element_type=F32)
        return carry

    lax.fori_loop(0, frames, forward, 0)
    spatial_out = jnp.where(live, acc[...], 0.0).astype(BF)
    sof[chans : 2 * chans] = spatial_out
    so_pair = frame_copies(
        sof.at[pl.ds(chans, chans)], sof.at[pl.ds(0, chans)], sof.at[pl.ds(2 * chans, chans)], 2
    )
    frame_start(so_pair)
    reduce_on(2, 1)

    gs_ext = ext[...].astype(BF)
    for fi in range(frames):
        z_part = lax.dot_general(
            weight((g_a, g_b), fi), gs_ext, contract_first, preferred_element_type=F32
        )
        zbuf[fi * sw : (fi + 1) * sw] = z_part[0:sw]
        if fi == 1:
            reduce_on(1, 2)
            reduce_on(2, 2)

    frame_arrived(so_pair)
    for fi in range(frames):
        piece = sof[fi * tw : fi * tw + tp]
        put((p_t,), fi, lax.dot_general(og_here, piece, contract_last, preferred_element_type=F32))
    reduce_start(0)

    def tap_sum(i, carry):
        r = pl.multiple_of(i * chunk, chunk)
        total_rows = jnp.zeros((chunk, cells), F32)
        for k in range(9):
            a, b = k // 3 - 1, k % 3 - 1
            s = a * COLUMNS + b
            rows = zbuf[pl.ds(pl.multiple_of(k * chans + r, 64), chunk)]
            rolled = pltpu.roll(rows, s % width, 1) if s else rows
            total_rows = total_rows + cut(rolled, -b)
        pre_rows = pre_ref[pl.ds(r, chunk)]
        sig = jax.nn.sigmoid(pre_rows)
        gpre_ref[pl.ds(r, chunk)] = jnp.where(
            live, total_rows * sig * (1.0 + pre_rows * (1.0 - sig)), 0.0
        )
        return carry

    lax.fori_loop(0, chans // chunk, tap_sum, 0)
    reduce_on(0, 1)
    stat = sums_start(
        1,
        [
            row_of(jnp.sum(gpre_ref[...] * normed_ref[...], axis=1, keepdims=True)),
            row_of(jnp.sum(gpre_ref[...], axis=1, keepdims=True)),
        ],
    )

    reduce_on(1, 3)
    reduce_on(2, 3)
    stat = sums_middle(1, stat)
    reduce_on(0, 2)
    reduce_on(1, 4)
    reduce_on(2, 4)
    sums = sums_end(1, stat)
    reduce_on(0, 3)

    scale = lax.rsqrt(count)
    chan_gain, chan_shift = sums[:, 0:chans], sums[:, stride : stride + chans]
    dgain[...] = scale * chan_gain
    dshift[...] = scale * chan_shift
    shift_sum = group_column(gain_row * chan_shift, group) / group_count
    gain_sum = group_column(gain_row * chan_gain, group) / group_count
    result = og[...].astype(F32) + rstd * (
        gain_column * gpre_ref[...] - shift_sum - normed_ref[...] * gain_sum
    )
    gi[...] = jnp.where(live, result, 0.0).astype(BF)

    reduce_on(0, 4)

    def finish(kind, out_stage):
        arrived(back[kind])
        block = partial[kind][c, zh, slot_own].astype(F32) + landing[4][kind][0].astype(F32)
        first, second = block[:own], block[own:]
        staged(out_stage, jnp.where(c == 0, second, first))
        return jnp.where(c == 0, first, second)

    mine, swaps = [None] * 3, [None] * 3
    ends = ((ys_t, yr_t), (ys_a, yr_a), (ys_b, yr_b))
    for kind in (1, 2, 0):
        mine[kind] = finish(kind, ends[kind][0])
        swaps[kind] = trade(1, kind, *ends[kind])
    for kind in (1, 2, 0):
        arrived(swaps[kind])
    theirs = [pair[1][0:own].astype(F32) for pair in ends]
    side_s = jnp.concatenate(mine[1:], axis=1), jnp.concatenate(theirs[1:], axis=1)
    for out, (a, b), wide in ((dws, side_s, sw), (dwt, (mine[0], theirs[0]), tw)):
        whole = jnp.concatenate([jnp.where(c == 0, a, b), jnp.where(c == 0, b, a)], axis=1)
        out[...] = scale * whole[:, 0:wide]

    for copy in pending:
        copy.wait_send()
    for pair in (og_pair, so_pair):
        frame_sent(pair)
    for pair in (act_pair, gs_pair):
        strip_sent(pair)


def hand_over(*refs):
    for source, target in zip(refs[:5], refs[5:]):
        target[...] = source[...].reshape(target.shape)


def fused(latents, out_grad, w_spatial, w_temporal, norm_gain, norm_shift, heights):
    chans, cells = latents.shape[1:]
    own, sw = w_spatial.shape
    tw = w_temporal.shape[1]
    pad = -(-own // 16) * 16
    th = -(-tw // 256) * 128
    sh = -(-sw // 256) * 128
    kinds = (th, sh - 128, 128)
    sp, tp = 2 * sh, 2 * th
    wide = -(-chans // 128) * 128

    scratch = (
        [pltpu.VMEM((2, 2, 8, 2 * own, kind), BF) for _ in range(2) for kind in kinds]
        + [
            pltpu.VMEM(lead + (2 * own, kind), BF)
            for lead in ((2, 8), (2, 4), (2, 2), (2, 1), (1,))
            for kind in kinds
        ]
        + [pltpu.VMEM((pad, kind), BF) for _ in range(4) for kind in kinds]
        + [
            pltpu.VMEM((2, chans, cells), BF),
            pltpu.VMEM((3 * chans + tp - tw, cells), BF),
            pltpu.VMEM((2, 2, chans, cells // 2), BF),
            pltpu.VMEM((2, 2, chans, cells // 2), BF),
            pltpu.VMEM((chans, 2 * cells), F32),
            pltpu.VMEM((9 * chans + sp - sw, cells), BF),
            pltpu.VMEM((9 * chans, 2 * cells), F32),
            pltpu.VMEM((chans, cells), F32),
        ]
        + [pltpu.VMEM((chans, cells), F32)] * 4
        + [
            pltpu.VMEM((2, 2, 1, 3 * wide), F32),
            pltpu.VMEM((2, 8, 1, 3 * wide), F32),
            pltpu.VMEM((2, 4, 1, 3 * wide), F32),
        ]
        + [pltpu.SemaphoreType.DMA((3, 8))] * 4
        + [pltpu.SemaphoreType.DMA((4,))] * 2
        + [pltpu.SemaphoreType.DMA((2, 2))] * 2
        + [pltpu.SemaphoreType.DMA((2, 12))] * 2
        + [pltpu.SemaphoreType.DMA((2, 3))] * 2
    )
    vmem = pl.BlockSpec(memory_space=pltpu.VMEM)
    outs = pl.pallas_call(
        whole_kernel,
        out_shape=(
            jax.ShapeDtypeStruct((chans, cells), BF),
            jax.ShapeDtypeStruct((own, sw), F32),
            jax.ShapeDtypeStruct((own, tw), F32),
            jax.ShapeDtypeStruct((1, chans), F32),
            jax.ShapeDtypeStruct((1, chans), F32),
        ),
        in_specs=[vmem] * 6 + [pl.BlockSpec(memory_space=pltpu.SMEM)],
        out_specs=(vmem,) * 5,
        scratch_shapes=scratch,
        compiler_params=pltpu.CompilerParams(
            collective_id=0, has_side_effects=True, vmem_limit_bytes=56 * 1024 * 1024
        ),
    )(
        latents[0], out_grad[0], w_spatial, w_temporal, norm_gain, norm_shift, heights
    )
    shapes = [outs[0].shape, outs[1].shape, outs[2].shape, (chans,), (chans,)]
    results = pl.pallas_call(
        hand_over,
        out_shape=tuple(
            jax.ShapeDtypeStruct(shape, out.dtype) for shape, out in zip(shapes, outs)
        ),
        in_specs=[vmem] * 5,
        out_specs=(vmem,) * 5,
    )(*outs)
    return (results[0][None],) + tuple(results[1:])


def solution(mesh):
    in_specs = (
        P("frame", None, "tile"),
        P("frame", None, "tile"),
        P("tile", "frame"),
        P("tile", "frame"),
        P(),
        P(),
        P("tile"),
    )
    out_specs = (P("frame", None, "tile"), P("tile", "frame"), P("tile", "frame"), P(), P())
    fits = mesh.shape["frame"] == 4 and mesh.shape["tile"] == 8
    return jax.shard_map(
        fused if fits else local, mesh=mesh, in_specs=in_specs, out_specs=out_specs, check_vma=False
    )
```

```python
import jax
import jax.numpy as jnp
from jax import lax
from jax.experimental import pallas as pl
from jax.experimental.pallas import tpu as pltpu
from jax.sharding import PartitionSpec as P

GROUPS = 32
COLUMNS = 16
STRIP_ROWS = 16


EPSILON = 1e-05


def from_behind(shard, axis, by):
    peers = lax.axis_size(axis)
    pairs = [(i, i + by) for i in range(peers) if 0 <= i + by < peers]
    return lax.ppermute(shard, axis, pairs)


def padded_2(cells, sides, width):
    for axis, dim in sides:
        count = lax.axis_size(axis)
        ends = count - 1
        head = lax.slice_in_dim(cells, 0, width, axis=dim)
        tail = lax.slice_in_dim(cells, cells.shape[dim] - width, cells.shape[dim], axis=dim)
        cells = jnp.concatenate(
            [
                lax.ppermute(tail, axis, [(i, (i + 1) % count) for i in range(ends)]),
                cells,
                lax.ppermute(head, axis, [((i + 1) % count, i) for i in range(ends)]),
            ],
            axis=dim,
        )
    return cells


def flip_taps(weight, tap_count):
    outputs = weight.shape[0]
    return jnp.transpose(weight.reshape(outputs, tap_count, -1)[:, ::-1, :], (2, 1, 0)).reshape(
        -1, tap_count * outputs
    )


def padded_rows(row_grid, above_row, below_row, height):
    channel_count = row_grid.shape[0]
    padded = jnp.zeros((channel_count, STRIP_ROWS + 2, COLUMNS + 2), row_grid.dtype)
    padded = padded.at[:, 1 : STRIP_ROWS + 1, 1 : COLUMNS + 1].set(row_grid)
    padded = padded.at[:, 0, 1 : COLUMNS + 1].set(above_row)
    below_block = jnp.pad(below_row, ((0, 0), (1, 1)))[:, None, :]
    return lax.dynamic_update_slice(padded, below_block, (jnp.int32(0), height + 1, jnp.int32(0)))


def tap_columns(padded, row_count):
    pieces = [
        padded[:, row_step : row_step + row_count, col_step : col_step + COLUMNS]
        for row_step in range(3)
        for col_step in range(3)
    ]
    return jnp.stack(pieces, axis=0).reshape(9 * padded.shape[0], row_count * COLUMNS)


def local(latents, out_grad, w_spatial, w_temporal, norm_gain, norm_shift, heights):
    channel_count = latents.shape[1]
    cell_count = latents.shape[2]
    group_size = channel_count // GROUPS
    height = heights[0]
    slot_row = jnp.arange(cell_count, dtype=jnp.int32) // COLUMNS
    live_cells = slot_row < height
    live_float = live_cells.astype(jnp.float32)
    contract_last = (((1,), (1,)), ((), ()))
    part_spatial_w, part_temporal_w = (
        lax.all_gather(w_spatial, "frame", axis=1, tiled=True),
        lax.all_gather(w_temporal, "frame", axis=1, tiled=True),
    )
    spatial_full, temporal_full = (
        lax.all_gather(part_spatial_w, "tile", axis=0, tiled=True),
        lax.all_gather(part_temporal_w, "tile", axis=0, tiled=True),
    )
    latent_full = latents[0].astype(jnp.float32)
    masked = latent_full * live_float[None, :]
    group_sum = masked.reshape(GROUPS, group_size, cell_count).sum(axis=(1, 2))
    group_square = (masked * latent_full).reshape(GROUPS, group_size, cell_count).sum(axis=(1, 2))
    own_count = height.astype(jnp.float32) * COLUMNS
    total_sum, total_square, position_count = lax.psum(
        (group_sum, group_square, own_count), ("frame", "tile")
    )
    group_count = position_count * group_size
    group_mean = total_sum / group_count
    group_rstd = lax.rsqrt(total_square / group_count - group_mean * group_mean + EPSILON)
    mean_column = jnp.repeat(group_mean, group_size)[:, None]
    rstd_column = jnp.repeat(group_rstd, group_size)[:, None]
    gain_column = norm_gain[:, None]
    normed = (latent_full - mean_column) * rstd_column
    pre_act = gain_column * normed + norm_shift[:, None]
    activated = jnp.where(live_cells[None, :], jax.nn.silu(pre_act), 0.0).astype(jnp.bfloat16)
    act_grid = activated.reshape(channel_count, STRIP_ROWS, COLUMNS)
    last_live = lax.dynamic_slice_in_dim(act_grid, height - 1, 1, 1)[:, 0, :]
    from_above = from_behind(last_live, "tile", 1)
    from_below = from_behind(act_grid[:, 0, :], "tile", -1)
    act_padded = padded_rows(act_grid, from_above, from_below, height)
    act_columns = tap_columns(act_padded, STRIP_ROWS)
    spatial_raw = jnp.dot(spatial_full, act_columns, preferred_element_type=jnp.float32)
    spatial_out = jnp.where(live_cells[None, :], spatial_raw, 0.0).astype(jnp.bfloat16)
    spatial_frames = padded_2(spatial_out[None], (("frame", 0),), 1)
    grad_here = jnp.where(live_cells[None, :], out_grad[0], jnp.zeros((), jnp.bfloat16))
    grad_frames = padded_2(grad_here[None], (("frame", 0),), 1)
    part_temporal = lax.dot_general(
        grad_here,
        spatial_frames.reshape(3 * channel_count, cell_count),
        contract_last,
        preferred_element_type=jnp.float32,
    )
    grad_spat = jnp.dot(
        flip_taps(temporal_full, 3),
        grad_frames.reshape(3 * channel_count, cell_count),
        preferred_element_type=jnp.float32,
    )
    grad_spat = jnp.where(live_cells[None, :], grad_spat, 0.0).astype(jnp.bfloat16)
    spat_grid = grad_spat.reshape(channel_count, STRIP_ROWS, COLUMNS)
    grad_last = lax.dynamic_slice_in_dim(spat_grid, height - 1, 1, 1)[:, 0, :]
    grad_above = from_behind(grad_last, "tile", 1)
    grad_below = from_behind(spat_grid[:, 0, :], "tile", -1)
    grad_padded = padded_rows(spat_grid, grad_above, grad_below, height)
    spatial_flip = flip_taps(spatial_full, 9)
    grad_act = jnp.dot(
        spatial_flip, tap_columns(grad_padded, STRIP_ROWS), preferred_element_type=jnp.float32
    )
    part_spatial = lax.dot_general(
        grad_spat, act_columns, contract_last, preferred_element_type=jnp.float32
    )
    sigmoid_act = jax.nn.sigmoid(pre_act)
    grad_pre = jnp.where(
        live_cells[None, :], grad_act * sigmoid_act * (1.0 + pre_act * (1.0 - sigmoid_act)), 0.0
    )
    chan_gain, chan_shift = lax.psum(
        (jnp.sum(grad_pre * normed, axis=1), jnp.sum(grad_pre, axis=1)), ("frame", "tile")
    )
    shift_sum = (norm_gain * chan_shift).reshape(GROUPS, group_size).sum(1) / group_count
    gain_sum = (norm_gain * chan_gain).reshape(GROUPS, group_size).sum(1) / group_count
    result = grad_here.astype(jnp.float32) + rstd_column * (
        gain_column * grad_pre
        - jnp.repeat(shift_sum, group_size)[:, None]
        - normed * jnp.repeat(gain_sum, group_size)[:, None]
    )
    grad_input = jnp.where(live_cells[None, :], result, 0.0).astype(jnp.bfloat16)[None]
    tile_spatial, tile_temporal = (
        lax.psum_scatter(
            part_spatial.astype(jnp.bfloat16), "tile", scatter_dimension=0, tiled=True
        ).astype(jnp.float32),
        lax.psum_scatter(
            part_temporal.astype(jnp.bfloat16), "tile", scatter_dimension=0, tiled=True
        ).astype(jnp.float32),
    )
    grad_spatial, grad_temporal = (
        lax.psum_scatter(
            tile_spatial.astype(jnp.bfloat16), "frame", scatter_dimension=1, tiled=True
        ).astype(jnp.float32),
        lax.psum_scatter(
            tile_temporal.astype(jnp.bfloat16), "frame", scatter_dimension=1, tiled=True
        ).astype(jnp.float32),
    )
    grad_scale = lax.rsqrt(position_count)
    return (
        grad_input,
        grad_scale * grad_spatial,
        grad_scale * grad_temporal,
        grad_scale * chan_gain,
        grad_scale * chan_shift,
    )


MESH = pl.DeviceIdType.MESH
BF = jnp.bfloat16
F32 = jnp.float32


def iota(shape, dim):
    return lax.broadcasted_iota(jnp.int32, shape, dim)


def group_of(n, size, dim):
    factor = (1 << 11) // size + 1
    return lax.shift_right_logical(iota((n, n), dim) * factor, 11)


def whole_kernel(
    lat, og, ws, wt, gain, shift, heights,
    gi, dws, dwt, dgain, dshift,
    g_t, g_a, g_b, p_t, p_a, p_b,
    r0t, r0a, r0b, r1t, r1a, r1b, r2t, r2a, r2b, r3t, r3a, r3b, r4t, r4a, r4b,
    xs_t, xs_a, xs_b, xr_t, xr_a, xr_b, ys_t, ys_a, ys_b, yr_t, yr_a, yr_b,
    ogf, sof, hsend, hrecv, ext, cols, zbuf, acc, normed_ref, pre_ref, gs_ref, gpre_ref,
    msg, tbuf, fbuf, eye_ref, same_ref,
    ag_send, ag_recv, rs_send, rs_recv, fr_send, fr_recv, ha_send, ha_recv, st_send, st_recv, tr_send, tr_recv,
):
    frames, tiles = 4, 8
    chans, cells = lat.shape
    own = ws.shape[0]
    lanes = tuple(buf.shape[4] for buf in (g_t, g_a, g_b))
    rows_in = 2 * own
    sp = 2 * (lanes[1] + lanes[2])
    tp = 2 * lanes[0]
    gathered, partial = (g_t, g_a, g_b), (p_t, p_a, p_b)
    landing = (
        (r0t, r0a, r0b), (r1t, r1a, r1b), (r2t, r2a, r2b), (r3t, r3a, r3b), (r4t, r4a, r4b),
    )
    sw, tw = ws.shape[1], wt.shape[1]
    group = chans // GROUPS
    f = lax.axis_index("frame")
    t = lax.axis_index("tile")
    y, x = f // 2, f % 2
    z, c = t // 2, t % 2
    zh, zl = z // 2, z % 2
    h = heights[0]
    live = iota((1, cells), 1) < h * COLUMNS
    short = h < STRIP_ROWS

    x_peer = (y * 2 + (1 - x), t)
    y_peer = ((1 - y) * 2 + x, t)
    z0_peer = (f, (zh * 2 + (1 - zl)) * 2 + c)
    z1_peer = (f, ((1 - zh) * 2 + zl) * 2 + c)
    c_peer = (f, z * 2 + (1 - c))

    barrier = pltpu.get_barrier_semaphore()
    for d in range(1, tiles):
        pl.semaphore_signal(barrier, inc=1, device_id=(f, (t + d) % tiles), device_id_type=MESH)
    for d in range(1, frames):
        pl.semaphore_signal(barrier, inc=1, device_id=((f + d) % frames, t), device_id_type=MESH)

    eye_ref[...] = jnp.where(iota((chans, chans), 0) == iota((chans, chans), 1), 1.0, 0.0)
    same_ref[...] = jnp.where(
        group_of(chans, group, 0) == group_of(chans, group, 1), 1.0, 0.0
    )

    def row_of(column):
        return jnp.sum(eye_ref[...] * column, axis=0, keepdims=True)

    def column_of(row):
        return jnp.sum(eye_ref[...] * row, axis=1, keepdims=True)

    def group_column(row):
        return jnp.sum(same_ref[...] * row, axis=1, keepdims=True)

    q_own = jnp.where(zh == 0, y, x)
    p_own = jnp.where(zh == 0, x, y)
    slot_own = q_own * 4 + p_own * 2 + zl
    def halves(src, wide):
        w32 = src[...].astype(F32)
        w32 = jnp.concatenate([w32, jnp.zeros((own, wide - w32.shape[1]), F32)], axis=1)
        first, second = w32[:, : wide // 2], w32[:, wide // 2 :]
        return jnp.where(c == 0, first, second), jnp.where(c == 0, second, first)

    kept_t, sent_t = halves(wt, tp)
    kept_s, sent_s = halves(ws, sp)
    kept = (kept_t, kept_s[:, : lanes[1]], kept_s[:, lanes[1] :])
    sent = (sent_t, sent_s[:, : lanes[1]], sent_s[:, lanes[1] :])

    def staged(ref, rows):
        ref[...] = jnp.concatenate(
            [rows, jnp.zeros((ref.shape[0] - own, rows.shape[1]), F32)], axis=0
        ).astype(BF)

    for ref, rows in zip((xs_t, xs_a, xs_b), sent):
        staged(ref, rows)
    masked = jnp.where(live, lat[...].astype(F32), 0.0)
    count_row = jnp.zeros((1, 128), F32) + h.astype(F32) * COLUMNS
    own_rows = [
        row_of(jnp.sum(masked, axis=1, keepdims=True)),
        row_of(jnp.sum(masked * masked, axis=1, keepdims=True)),
        count_row,
    ]
    gain_row = gain[...].reshape(1, chans)
    gain_column = column_of(gain_row)
    shift_column = column_of(shift[...].reshape(1, chans))
    pl.semaphore_wait(barrier, tiles + frames - 2)

    pending = []

    def remote(src, dst, ss, rs, peer):
        copy = pltpu.make_async_remote_copy(
            src_ref=src, dst_ref=dst, send_sem=ss, recv_sem=rs, device_id=peer, device_id_type=MESH
        )
        copy.start()
        pending.append(copy)
        return copy

    def trade(which, kind, src, dst):
        return [
            remote(src, dst, tr_send.at[which, kind], tr_recv.at[which, kind], c_peer)
        ]

    def gather_step(kind, step):
        buf = gathered[kind]
        if step == 0:
            moves = [(0, (c, zh, pl.ds(slot_own, 1)), z1_peer)]
        elif step == 1:
            moves = [
                (1, (c, 0, pl.ds(y * 4 + x * 2 + zl, 1)), z0_peer),
                (2, (c, 1, pl.ds(x * 4 + y * 2 + zl, 1)), z0_peer),
            ]
        elif step == 2:
            moves = [
                (3, (c, 0, pl.ds(y * 4 + x * 2, 2)), x_peer),
                (4, (c, 1, pl.ds(x * 4 + y * 2, 2)), y_peer),
            ]
        elif step == 3:
            moves = [
                (5, (c, 0, pl.ds(y * 4, 4)), y_peer),
                (6, (c, 1, pl.ds(x * 4, 4)), x_peer),
            ]
        else:
            moves = [(7, (c,), c_peer)]
        return [
            remote(buf.at[at], buf.at[at], ag_send.at[kind, i], ag_recv.at[kind, i], peer)
            for i, at, peer in moves
        ]

    def arrived(copies):
        for copy in copies:
            copy.wait_recv()

    def frame_copies(src, prev_dst, next_dst, base):
        up = pltpu.make_async_remote_copy(
            src_ref=src, dst_ref=prev_dst, send_sem=fr_send.at[base], recv_sem=fr_recv.at[base],
            device_id=((f + 1) % frames, t), device_id_type=MESH,
        )
        down = pltpu.make_async_remote_copy(
            src_ref=src, dst_ref=next_dst, send_sem=fr_send.at[base + 1], recv_sem=fr_recv.at[base + 1],
            device_id=((f + frames - 1) % frames, t), device_id_type=MESH,
        )
        return up, down

    def frame_start(pair):
        pl.when(f < frames - 1)(lambda: pair[0].start())
        pl.when(f > 0)(lambda: pair[1].start())

    def frame_arrived(pair):
        pl.when(f > 0)(lambda: pair[0].wait_recv())
        pl.when(f < frames - 1)(lambda: pair[1].wait_recv())

    def frame_sent(pair):
        pl.when(f < frames - 1)(lambda: pair[0].wait_send())
        pl.when(f > 0)(lambda: pair[1].wait_send())

    def strip_copies(which):
        down = pltpu.make_async_remote_copy(
            src_ref=hsend.at[which, 0], dst_ref=hrecv.at[which, 0],
            send_sem=ha_send.at[which, 0], recv_sem=ha_recv.at[which, 0],
            device_id=(f, (t + 1) % tiles), device_id_type=MESH,
        )
        up = pltpu.make_async_remote_copy(
            src_ref=hsend.at[which, 1], dst_ref=hrecv.at[which, 1],
            send_sem=ha_send.at[which, 1], recv_sem=ha_recv.at[which, 1],
            device_id=(f, (t + tiles - 1) % tiles), device_id_type=MESH,
        )
        return down, up

    def strip_start(pair, which, grid):
        half = cells // 2
        hsend[which, 0] = jnp.where(short, grid[:, :half], grid[:, half:]).astype(BF)
        hsend[which, 1] = grid[:, :half].astype(BF)
        pl.when(t < tiles - 1)(lambda: pair[0].start())
        pl.when(t > 0)(lambda: pair[1].start())

    def strip_arrived(pair):
        pl.when(t > 0)(lambda: pair[0].wait_recv())
        pl.when(t < tiles - 1)(lambda: pair[1].wait_recv())

    def strip_sent(pair):
        pl.when(t < tiles - 1)(lambda: pair[0].wait_send())
        pl.when(t > 0)(lambda: pair[1].wait_send())

    def strip_extended(which, grid):
        half = cells // 2
        above = hrecv[which, 0].astype(F32)
        below = hrecv[which, 1].astype(F32)
        return jnp.concatenate(
            [above, grid[:, :half], jnp.where(short, below, grid[:, half:]), below], axis=1
        )

    stride = msg.shape[3] // 3

    def sums_start(which, rows):
        row = jnp.zeros((1, msg.shape[3]), F32)
        for i, part in enumerate(rows):
            at = i * stride
            row_parts = [jnp.zeros((1, at), F32)] if at else []
            row_parts.append(part)
            rest = msg.shape[3] - at - part.shape[1]
            if rest:
                row_parts.append(jnp.zeros((1, rest), F32))
            row = row + jnp.concatenate(row_parts, axis=1)
        msg[which, 0] = row
        tbuf[which, t] = msg[which, 0]
        return [
            remote(
                msg.at[which, 0], tbuf.at[which, t], st_send.at[which, d], st_recv.at[which, d],
                (f, (t + d) % tiles),
            )
            for d in range(1, tiles)
        ]

    def sums_middle(which, copies):
        arrived(copies)
        total = tbuf[which, 0]
        for i in range(1, tiles):
            total = total + tbuf[which, i]
        msg[which, 1] = total
        fbuf[which, f] = total
        return [
            remote(
                msg.at[which, 1], fbuf.at[which, f], st_send.at[which, tiles + d],
                st_recv.at[which, tiles + d], ((f + d) % frames, t),
            )
            for d in range(1, frames)
        ]

    def sums_end(which, copies):
        arrived(copies)
        total = fbuf[which, 0]
        for i in range(1, frames):
            total = total + fbuf[which, i]
        return total

    stat = sums_start(0, own_rows)
    traded = [
        trade(0, kind, src, dst)
        for kind, (src, dst) in enumerate(((xs_t, xr_t), (xs_a, xr_a), (xs_b, xr_b)))
    ]
    og_pair = frame_copies(og, ogf.at[0], ogf.at[1], 0)
    frame_start(og_pair)

    @pl.when(f == 0)
    def _():
        ogf[0] = jnp.zeros_like(ogf[0])
        sof[0:chans] = jnp.zeros((chans, cells), BF)

    @pl.when(f == frames - 1)
    def _():
        ogf[1] = jnp.zeros_like(ogf[1])
        sof[2 * chans : 3 * chans] = jnp.zeros((chans, cells), BF)

    @pl.when(t == 0)
    def _():
        hrecv[0, 0] = jnp.zeros_like(hrecv[0, 0])
        hrecv[1, 0] = jnp.zeros_like(hrecv[1, 0])

    @pl.when(t == tiles - 1)
    def _():
        hrecv[0, 1] = jnp.zeros_like(hrecv[0, 1])
        hrecv[1, 1] = jnp.zeros_like(hrecv[1, 1])

    sof[3 * chans :] = jnp.zeros((sof.shape[0] - 3 * chans, cells), BF)
    cols[9 * chans :] = jnp.zeros((cols.shape[0] - 9 * chans, cells), BF)

    chain = [None] * 3
    for kind, ref in enumerate((xr_t, xr_a, xr_b)):
        arrived(traded[kind])
        other = ref[0:own].astype(F32)
        gathered[kind][c, zh, slot_own] = jnp.concatenate(
            [jnp.where(c == 0, kept[kind], other), jnp.where(c == 0, other, kept[kind])], axis=0
        ).astype(BF)
        chain[kind] = gather_step(kind, 0)

    def forth(kind, step):
        arrived(chain[kind])
        if step < 5:
            chain[kind] = gather_step(kind, step)

    stat = sums_middle(0, stat)
    forth(0, 1)
    total = sums_end(0, stat)
    count = total[:, 2 * stride : 2 * stride + 1]
    group_count = count * group
    mean = group_column(total[:, 0:chans]) / group_count
    rstd = lax.rsqrt(
        group_column(total[:, stride : stride + chans]) / group_count - mean * mean + EPSILON
    )
    normed = (lat[...].astype(F32) - mean) * rstd
    pre = gain_column * normed + shift_column
    normed_ref[...] = normed
    pre_ref[...] = pre
    act = jnp.where(live, pre * jax.nn.sigmoid(pre), 0.0).astype(BF).astype(F32)
    act_pair = strip_copies(0)
    strip_start(act_pair, 0, act)
    forth(1, 1)
    forth(2, 1)
    forth(0, 2)
    frame_arrived(og_pair)
    og_here = jnp.where(live, og[...], jnp.zeros((), BF))
    og_next = jnp.where(live, ogf[1], jnp.zeros((), BF))
    og_prev = jnp.where(live, ogf[0], jnp.zeros((), BF))
    forth(1, 2)
    forth(2, 2)
    forth(0, 3)
    strip_arrived(act_pair)
    ext[...] = strip_extended(0, act)

    width = ext.shape[1]
    chunk = 64
    col = iota((1, cells), 1) % COLUMNS
    left_ok = col >= 1
    right_ok = col < COLUMNS - 1
    half = cells // 2

    def cut(rolled, b):
        piece = rolled[:, half : half + cells]
        if b < 0:
            piece = jnp.where(left_ok, piece, 0.0)
        if b > 0:
            piece = jnp.where(right_ok, piece, 0.0)
        return piece

    def tap_rows(i, carry):
        r = pl.multiple_of(i * chunk, chunk)
        rows = ext[pl.ds(r, chunk)]
        for k in range(9):
            a, b = k // 3 - 1, k % 3 - 1
            s = a * COLUMNS + b
            rolled = pltpu.roll(rows, (-s) % width, 1) if s else rows
            cols[pl.ds(pl.multiple_of(k * chans + r, 64), chunk)] = cut(rolled, b).astype(BF)
        return carry

    lax.fori_loop(0, 2, tap_rows, 0)
    forth(0, 4)
    forth(1, 3)
    lax.fori_loop(2, chans // chunk, tap_rows, 0)
    forth(2, 3)

    def slots(fi):
        yi, xi = fi // 2, fi % 2
        return yi * 4 + xi * 2, xi * 4 + yi * 2

    def weight(bufs, fi):
        at = slots(fi)
        sides = []
        for side in range(2):
            for buf in bufs:
                sides.append(
                    jnp.concatenate(
                        [buf[side, zi // 2, at[zi // 2] + zi % 2] for zi in range(4)], axis=0
                    )
                )
        return jnp.concatenate(sides, axis=1)

    def put(bufs, fi, value):
        at = slots(fi)
        lane = 0
        for side in range(2):
            for buf in bufs:
                wide = buf.shape[4]
                for zi in range(4):
                    buf[side, zi // 2, at[zi // 2] + zi % 2] = value[
                        zi * rows_in : (zi + 1) * rows_in, lane : lane + wide
                    ].astype(BF)
                lane += wide

    contract_first = (((0,), (0,)), ((), ()))
    contract_last = (((1,), (1,)), ((), ()))

    forth(0, 5)
    windows = (og_next, og_here, og_prev)
    for fi in range(frames):
        block = weight((g_t,), fi)
        lo, hi = fi * tw, (fi + 1) * tw
        taps = [k for k in range(3) if max(lo, k * chans) < min(hi, (k + 1) * chans)]
        window = jnp.concatenate([windows[k] for k in taps], axis=1)
        part = lax.dot_general(block, window, contract_first, preferred_element_type=F32)
        for i, k in enumerate(taps):
            first, last = max(lo, k * chans), min(hi, (k + 1) * chans)
            zbuf[first:last, 0:cells] = part[first - lo : last - lo, i * cells : (i + 1) * cells]
    gs = zbuf[0:chans, 0:cells] + zbuf[chans : 2 * chans, 0:cells]
    gs = gs + zbuf[2 * chans : 3 * chans, 0:cells]
    gs = jnp.where(live, gs, 0.0).astype(BF).astype(F32)
    gs_ref[...] = gs
    gs_pair = strip_copies(1)
    strip_start(gs_pair, 1, gs)

    def spatial_terms(fi, carry):
        here = gs_ref[...].astype(BF)
        piece = cols[pl.ds(pl.multiple_of(fi * sw, 16), sp)]
        put((p_a, p_b), fi, lax.dot_general(here, piece, contract_last, preferred_element_type=F32))
        return carry

    lax.fori_loop(0, frames, spatial_terms, 0)

    def reduce_step(kind, step):
        buf = partial[kind]
        into = landing[step][kind]
        if step == 0:
            moves = [(0, (1 - c,), into, c_peer)]
        elif step == 1:
            moves = [
                (1, (c, 0, pl.ds((1 - y) * 4, 4)), into.at[0], y_peer),
                (2, (c, 1, pl.ds((1 - x) * 4, 4)), into.at[1], x_peer),
            ]
        elif step == 2:
            moves = [
                (3, (c, 0, pl.ds(y * 4 + (1 - x) * 2, 2)), into.at[0], x_peer),
                (4, (c, 1, pl.ds(x * 4 + (1 - y) * 2, 2)), into.at[1], y_peer),
            ]
        elif step == 3:
            moves = [
                (5, (c, 0, pl.ds(y * 4 + x * 2 + (1 - zl), 1)), into.at[0], z0_peer),
                (6, (c, 1, pl.ds(x * 4 + y * 2 + (1 - zl), 1)), into.at[1], z0_peer),
            ]
        else:
            q = jnp.where(zh == 0, x, y)
            p = jnp.where(zh == 0, y, x)
            moves = [(7, (c, 1 - zh, pl.ds(q * 4 + p * 2 + zl, 1)), into, z1_peer)]
        return [
            remote(buf.at[at], dst, rs_send.at[kind, i], rs_recv.at[kind, i], peer)
            for i, at, dst, peer in moves
        ]

    def reduce_add(kind, step):
        buf = partial[kind]
        into = landing[step][kind]
        blocks = (8, 4, 2, 1)[step]
        starts = (
            (0, 0),
            (y * 4, x * 4),
            (y * 4 + x * 2, x * 4 + y * 2),
            (y * 4 + x * 2 + zl, x * 4 + y * 2 + zl),
        )[step]
        for hi in range(2):
            def add(i, carry):
                here = buf[c, hi, starts[hi] + i].astype(F32) + into[hi, i].astype(F32)
                buf[c, hi, starts[hi] + i] = here.astype(BF)
                return carry

            lax.fori_loop(0, blocks, add, 0)

    back = [None] * 3

    def reduce_start(kind):
        back[kind] = reduce_step(kind, 0)

    def reduce_on(kind, step):
        arrived(back[kind])
        reduce_add(kind, step - 1)
        back[kind] = reduce_step(kind, step)

    forth(1, 4)
    forth(2, 4)
    reduce_start(1)
    reduce_start(2)
    strip_arrived(gs_pair)
    ext[...] = strip_extended(1, gs_ref[...])
    forth(1, 5)
    forth(2, 5)
    reduce_on(1, 1)

    acc[...] = jnp.zeros_like(acc)

    def forward(fi, carry):
        piece = cols[pl.ds(pl.multiple_of(fi * sw, 16), sp)]
        acc[...] += jnp.dot(weight((g_a, g_b), fi), piece, preferred_element_type=F32)
        return carry

    lax.fori_loop(0, frames, forward, 0)
    spatial_out = jnp.where(live, acc[...], 0.0).astype(BF)
    sof[chans : 2 * chans] = spatial_out
    so_pair = frame_copies(
        sof.at[pl.ds(chans, chans)], sof.at[pl.ds(0, chans)], sof.at[pl.ds(2 * chans, chans)], 2
    )
    frame_start(so_pair)
    reduce_on(2, 1)

    gs_ext = ext[...].astype(BF)
    for fi in range(frames):
        z_part = lax.dot_general(
            weight((g_a, g_b), fi), gs_ext, contract_first, preferred_element_type=F32
        )
        zbuf[fi * sw : (fi + 1) * sw] = z_part[0:sw]
        if fi == 1:
            reduce_on(1, 2)
            reduce_on(2, 2)

    frame_arrived(so_pair)
    for fi in range(frames):
        piece = sof[fi * tw : fi * tw + tp]
        put((p_t,), fi, lax.dot_general(og_here, piece, contract_last, preferred_element_type=F32))
    reduce_start(0)

    def tap_sum(i, carry):
        r = pl.multiple_of(i * chunk, chunk)
        total_rows = jnp.zeros((chunk, cells), F32)
        for k in range(9):
            a, b = k // 3 - 1, k % 3 - 1
            s = a * COLUMNS + b
            rows = zbuf[pl.ds(pl.multiple_of(k * chans + r, 64), chunk)]
            rolled = pltpu.roll(rows, s % width, 1) if s else rows
            total_rows = total_rows + cut(rolled, -b)
        pre_rows = pre_ref[pl.ds(r, chunk)]
        sig = jax.nn.sigmoid(pre_rows)
        gpre_ref[pl.ds(r, chunk)] = jnp.where(
            live, total_rows * sig * (1.0 + pre_rows * (1.0 - sig)), 0.0
        )
        return carry

    lax.fori_loop(0, 1, tap_sum, 0)
    reduce_on(0, 1)
    lax.fori_loop(1, 2, tap_sum, 0)
    reduce_on(1, 3)
    reduce_on(2, 3)
    lax.fori_loop(2, 3, tap_sum, 0)
    reduce_on(0, 2)
    lax.fori_loop(3, 4, tap_sum, 0)
    reduce_on(1, 4)
    reduce_on(2, 4)
    lax.fori_loop(4, chans // chunk, tap_sum, 0)
    reduce_on(0, 3)
    stat = sums_start(
        1,
        [
            row_of(jnp.sum(gpre_ref[...] * normed_ref[...], axis=1, keepdims=True)),
            row_of(jnp.sum(gpre_ref[...], axis=1, keepdims=True)),
        ],
    )

    def finish(kind, out_stage):
        arrived(back[kind])
        block = partial[kind][c, zh, slot_own].astype(F32) + landing[4][kind][0].astype(F32)
        first, second = block[:own], block[own:]
        staged(out_stage, jnp.where(c == 0, second, first))
        return jnp.where(c == 0, first, second)

    mine, swaps = [None] * 3, [None] * 3
    ends = ((ys_t, yr_t), (ys_a, yr_a), (ys_b, yr_b))
    for kind in (1, 2):
        mine[kind] = finish(kind, ends[kind][0])
        swaps[kind] = trade(1, kind, *ends[kind])
    stat = sums_middle(1, stat)
    reduce_on(0, 4)
    sums = sums_end(1, stat)

    scale = lax.rsqrt(count)
    chan_gain, chan_shift = sums[:, 0:chans], sums[:, stride : stride + chans]
    dgain[...] = scale * chan_gain
    dshift[...] = scale * chan_shift
    shift_sum = group_column(gain_row * chan_shift) / group_count
    gain_sum = group_column(gain_row * chan_gain) / group_count
    result = og[...].astype(F32) + rstd * (
        gain_column * gpre_ref[...] - shift_sum - normed_ref[...] * gain_sum
    )
    gi[...] = jnp.where(live, result, 0.0).astype(BF)

    mine[0] = finish(0, ends[0][0])
    swaps[0] = trade(1, 0, *ends[0])
    for kind in (1, 2, 0):
        arrived(swaps[kind])
    theirs = [pair[1][0:own].astype(F32) for pair in ends]
    side_s = jnp.concatenate(mine[1:], axis=1), jnp.concatenate(theirs[1:], axis=1)
    for out, (a, b), wide in ((dws, side_s, sw), (dwt, (mine[0], theirs[0]), tw)):
        whole = jnp.concatenate([jnp.where(c == 0, a, b), jnp.where(c == 0, b, a)], axis=1)
        out[...] = scale * whole[:, 0:wide]

    for copy in pending:
        copy.wait_send()
    for pair in (og_pair, so_pair):
        frame_sent(pair)
    for pair in (act_pair, gs_pair):
        strip_sent(pair)


def hand_over(*refs):
    for source, target in zip(refs[:5], refs[5:]):
        target[...] = source[...].reshape(target.shape)


def fused(latents, out_grad, w_spatial, w_temporal, norm_gain, norm_shift, heights):
    chans, cells = latents.shape[1:]
    own, sw = w_spatial.shape
    tw = w_temporal.shape[1]
    pad = -(-own // 16) * 16
    th = -(-tw // 256) * 128
    sh = -(-sw // 256) * 128
    kinds = (th, sh - 128, 128)
    sp, tp = 2 * sh, 2 * th
    wide = -(-chans // 128) * 128

    scratch = (
        [pltpu.VMEM((2, 2, 8, 2 * own, kind), BF) for _ in range(2) for kind in kinds]
        + [
            pltpu.VMEM(lead + (2 * own, kind), BF)
            for lead in ((2, 8), (2, 4), (2, 2), (2, 1), (1,))
            for kind in kinds
        ]
        + [pltpu.VMEM((pad, kind), BF) for _ in range(4) for kind in kinds]
        + [
            pltpu.VMEM((2, chans, cells), BF),
            pltpu.VMEM((3 * chans + tp - tw, cells), BF),
            pltpu.VMEM((2, 2, chans, cells // 2), BF),
            pltpu.VMEM((2, 2, chans, cells // 2), BF),
            pltpu.VMEM((chans, 2 * cells), F32),
            pltpu.VMEM((9 * chans + sp - sw, cells), BF),
            pltpu.VMEM((9 * chans, 2 * cells), F32),
            pltpu.VMEM((chans, cells), F32),
        ]
        + [pltpu.VMEM((chans, cells), F32)] * 4
        + [
            pltpu.VMEM((2, 2, 1, 3 * wide), F32),
            pltpu.VMEM((2, 8, 1, 3 * wide), F32),
            pltpu.VMEM((2, 4, 1, 3 * wide), F32),
            pltpu.VMEM((chans, chans), F32),
            pltpu.VMEM((chans, chans), F32),
        ]
        + [pltpu.SemaphoreType.DMA((3, 8))] * 4
        + [pltpu.SemaphoreType.DMA((4,))] * 2
        + [pltpu.SemaphoreType.DMA((2, 2))] * 2
        + [pltpu.SemaphoreType.DMA((2, 12))] * 2
        + [pltpu.SemaphoreType.DMA((2, 3))] * 2
    )
    vmem = pl.BlockSpec(memory_space=pltpu.VMEM)
    outs = pl.pallas_call(
        whole_kernel,
        out_shape=(
            jax.ShapeDtypeStruct((chans, cells), BF),
            jax.ShapeDtypeStruct((own, sw), F32),
            jax.ShapeDtypeStruct((own, tw), F32),
            jax.ShapeDtypeStruct((1, chans), F32),
            jax.ShapeDtypeStruct((1, chans), F32),
        ),
        in_specs=[vmem] * 6 + [pl.BlockSpec(memory_space=pltpu.SMEM)],
        out_specs=(vmem,) * 5,
        scratch_shapes=scratch,
        compiler_params=pltpu.CompilerParams(
            collective_id=0, has_side_effects=True, vmem_limit_bytes=56 * 1024 * 1024
        ),
    )(
        latents[0], out_grad[0], w_spatial, w_temporal, norm_gain, norm_shift, heights
    )
    shapes = [outs[0].shape, outs[1].shape, outs[2].shape, (chans,), (chans,)]
    results = pl.pallas_call(
        hand_over,
        out_shape=tuple(
            jax.ShapeDtypeStruct(shape, out.dtype) for shape, out in zip(shapes, outs)
        ),
        in_specs=[vmem] * 5,
        out_specs=(vmem,) * 5,
    )(*outs)
    return (results[0][None],) + tuple(results[1:])


def solution(mesh):
    in_specs = (
        P("frame", None, "tile"),
        P("frame", None, "tile"),
        P("tile", "frame"),
        P("tile", "frame"),
        P(),
        P(),
        P("tile"),
    )
    out_specs = (P("frame", None, "tile"), P("tile", "frame"), P("tile", "frame"), P(), P())
    fits = mesh.shape["frame"] == 4 and mesh.shape["tile"] == 8
    return jax.shard_map(
        fused if fits else local, mesh=mesh, in_specs=in_specs, out_specs=out_specs, check_vma=False
    )
```

```python
import jax
import jax.numpy as jnp
from jax import lax
from jax.experimental import pallas as pl
from jax.experimental.pallas import tpu as pltpu
from jax.sharding import PartitionSpec as P

GROUPS = 32
COLUMNS = 16
STRIP_ROWS = 16


EPSILON = 1e-05


def from_behind(shard, axis, by):
    peers = lax.axis_size(axis)
    pairs = [(i, i + by) for i in range(peers) if 0 <= i + by < peers]
    return lax.ppermute(shard, axis, pairs)


def padded_2(cells, sides, width):
    for axis, dim in sides:
        count = lax.axis_size(axis)
        ends = count - 1
        head = lax.slice_in_dim(cells, 0, width, axis=dim)
        tail = lax.slice_in_dim(cells, cells.shape[dim] - width, cells.shape[dim], axis=dim)
        cells = jnp.concatenate(
            [
                lax.ppermute(tail, axis, [(i, (i + 1) % count) for i in range(ends)]),
                cells,
                lax.ppermute(head, axis, [((i + 1) % count, i) for i in range(ends)]),
            ],
            axis=dim,
        )
    return cells


def flip_taps(weight, tap_count):
    outputs = weight.shape[0]
    return jnp.transpose(weight.reshape(outputs, tap_count, -1)[:, ::-1, :], (2, 1, 0)).reshape(
        -1, tap_count * outputs
    )


def padded_rows(row_grid, above_row, below_row, height):
    channel_count = row_grid.shape[0]
    padded = jnp.zeros((channel_count, STRIP_ROWS + 2, COLUMNS + 2), row_grid.dtype)
    padded = padded.at[:, 1 : STRIP_ROWS + 1, 1 : COLUMNS + 1].set(row_grid)
    padded = padded.at[:, 0, 1 : COLUMNS + 1].set(above_row)
    below_block = jnp.pad(below_row, ((0, 0), (1, 1)))[:, None, :]
    return lax.dynamic_update_slice(padded, below_block, (jnp.int32(0), height + 1, jnp.int32(0)))


def tap_columns(padded, row_count):
    pieces = [
        padded[:, row_step : row_step + row_count, col_step : col_step + COLUMNS]
        for row_step in range(3)
        for col_step in range(3)
    ]
    return jnp.stack(pieces, axis=0).reshape(9 * padded.shape[0], row_count * COLUMNS)


def local(latents, out_grad, w_spatial, w_temporal, norm_gain, norm_shift, heights):
    channel_count = latents.shape[1]
    cell_count = latents.shape[2]
    group_size = channel_count // GROUPS
    height = heights[0]
    slot_row = jnp.arange(cell_count, dtype=jnp.int32) // COLUMNS
    live_cells = slot_row < height
    live_float = live_cells.astype(jnp.float32)
    contract_last = (((1,), (1,)), ((), ()))
    part_spatial_w, part_temporal_w = (
        lax.all_gather(w_spatial, "frame", axis=1, tiled=True),
        lax.all_gather(w_temporal, "frame", axis=1, tiled=True),
    )
    spatial_full, temporal_full = (
        lax.all_gather(part_spatial_w, "tile", axis=0, tiled=True),
        lax.all_gather(part_temporal_w, "tile", axis=0, tiled=True),
    )
    latent_full = latents[0].astype(jnp.float32)
    masked = latent_full * live_float[None, :]
    group_sum = masked.reshape(GROUPS, group_size, cell_count).sum(axis=(1, 2))
    group_square = (masked * latent_full).reshape(GROUPS, group_size, cell_count).sum(axis=(1, 2))
    own_count = height.astype(jnp.float32) * COLUMNS
    total_sum, total_square, position_count = lax.psum(
        (group_sum, group_square, own_count), ("frame", "tile")
    )
    group_count = position_count * group_size
    group_mean = total_sum / group_count
    group_rstd = lax.rsqrt(total_square / group_count - group_mean * group_mean + EPSILON)
    mean_column = jnp.repeat(group_mean, group_size)[:, None]
    rstd_column = jnp.repeat(group_rstd, group_size)[:, None]
    gain_column = norm_gain[:, None]
    normed = (latent_full - mean_column) * rstd_column
    pre_act = gain_column * normed + norm_shift[:, None]
    activated = jnp.where(live_cells[None, :], jax.nn.silu(pre_act), 0.0).astype(jnp.bfloat16)
    act_grid = activated.reshape(channel_count, STRIP_ROWS, COLUMNS)
    last_live = lax.dynamic_slice_in_dim(act_grid, height - 1, 1, 1)[:, 0, :]
    from_above = from_behind(last_live, "tile", 1)
    from_below = from_behind(act_grid[:, 0, :], "tile", -1)
    act_padded = padded_rows(act_grid, from_above, from_below, height)
    act_columns = tap_columns(act_padded, STRIP_ROWS)
    spatial_raw = jnp.dot(spatial_full, act_columns, preferred_element_type=jnp.float32)
    spatial_out = jnp.where(live_cells[None, :], spatial_raw, 0.0).astype(jnp.bfloat16)
    spatial_frames = padded_2(spatial_out[None], (("frame", 0),), 1)
    grad_here = jnp.where(live_cells[None, :], out_grad[0], jnp.zeros((), jnp.bfloat16))
    grad_frames = padded_2(grad_here[None], (("frame", 0),), 1)
    part_temporal = lax.dot_general(
        grad_here,
        spatial_frames.reshape(3 * channel_count, cell_count),
        contract_last,
        preferred_element_type=jnp.float32,
    )
    grad_spat = jnp.dot(
        flip_taps(temporal_full, 3),
        grad_frames.reshape(3 * channel_count, cell_count),
        preferred_element_type=jnp.float32,
    )
    grad_spat = jnp.where(live_cells[None, :], grad_spat, 0.0).astype(jnp.bfloat16)
    spat_grid = grad_spat.reshape(channel_count, STRIP_ROWS, COLUMNS)
    grad_last = lax.dynamic_slice_in_dim(spat_grid, height - 1, 1, 1)[:, 0, :]
    grad_above = from_behind(grad_last, "tile", 1)
    grad_below = from_behind(spat_grid[:, 0, :], "tile", -1)
    grad_padded = padded_rows(spat_grid, grad_above, grad_below, height)
    spatial_flip = flip_taps(spatial_full, 9)
    grad_act = jnp.dot(
        spatial_flip, tap_columns(grad_padded, STRIP_ROWS), preferred_element_type=jnp.float32
    )
    part_spatial = lax.dot_general(
        grad_spat, act_columns, contract_last, preferred_element_type=jnp.float32
    )
    sigmoid_act = jax.nn.sigmoid(pre_act)
    grad_pre = jnp.where(
        live_cells[None, :], grad_act * sigmoid_act * (1.0 + pre_act * (1.0 - sigmoid_act)), 0.0
    )
    chan_gain, chan_shift = lax.psum(
        (jnp.sum(grad_pre * normed, axis=1), jnp.sum(grad_pre, axis=1)), ("frame", "tile")
    )
    shift_sum = (norm_gain * chan_shift).reshape(GROUPS, group_size).sum(1) / group_count
    gain_sum = (norm_gain * chan_gain).reshape(GROUPS, group_size).sum(1) / group_count
    result = grad_here.astype(jnp.float32) + rstd_column * (
        gain_column * grad_pre
        - jnp.repeat(shift_sum, group_size)[:, None]
        - normed * jnp.repeat(gain_sum, group_size)[:, None]
    )
    grad_input = jnp.where(live_cells[None, :], result, 0.0).astype(jnp.bfloat16)[None]
    tile_spatial, tile_temporal = (
        lax.psum_scatter(
            part_spatial.astype(jnp.bfloat16), "tile", scatter_dimension=0, tiled=True
        ).astype(jnp.float32),
        lax.psum_scatter(
            part_temporal.astype(jnp.bfloat16), "tile", scatter_dimension=0, tiled=True
        ).astype(jnp.float32),
    )
    grad_spatial, grad_temporal = (
        lax.psum_scatter(
            tile_spatial.astype(jnp.bfloat16), "frame", scatter_dimension=1, tiled=True
        ).astype(jnp.float32),
        lax.psum_scatter(
            tile_temporal.astype(jnp.bfloat16), "frame", scatter_dimension=1, tiled=True
        ).astype(jnp.float32),
    )
    grad_scale = lax.rsqrt(position_count)
    return (
        grad_input,
        grad_scale * grad_spatial,
        grad_scale * grad_temporal,
        grad_scale * chan_gain,
        grad_scale * chan_shift,
    )


MESH = pl.DeviceIdType.MESH
BF = jnp.bfloat16
F32 = jnp.float32


def iota(shape, dim):
    return lax.broadcasted_iota(jnp.int32, shape, dim)


def group_of(n, size, dim):
    factor = (1 << 11) // size + 1
    return lax.shift_right_logical(iota((n, n), dim) * factor, 11)


def whole_kernel(
    lat, og, ws, wt, gain, shift, heights,
    gi, dws, dwt, dgain, dshift,
    g_t, g_a, g_b, p_t, p_a, p_b,
    r0t, r0a, r0b, r1t, r1a, r1b, r2t, r2a, r2b, r3t, r3a, r3b, r4t, r4a, r4b,
    xs_t, xs_a, xs_b, xr_t, xr_a, xr_b, ys_t, ys_a, ys_b, yr_t, yr_a, yr_b,
    ogf, sof, hsend, hrecv, ext, cols, zbuf, acc, normed_ref, pre_ref, gs_ref, gpre_ref,
    msg, tbuf, fbuf, eye_ref, same_ref,
    ag_send, ag_recv, rs_send, rs_recv, fr_send, fr_recv, ha_send, ha_recv, st_send, st_recv, tr_send, tr_recv,
):
    frames, tiles = 4, 8
    chans, cells = lat.shape
    own = ws.shape[0]
    lanes = tuple(buf.shape[4] for buf in (g_t, g_a, g_b))
    rows_in = 2 * own
    sp = 2 * (lanes[1] + lanes[2])
    tp = 2 * lanes[0]
    gathered, partial = (g_t, g_a, g_b), (p_t, p_a, p_b)
    landing = (
        (r0t, r0a, r0b), (r1t, r1a, r1b), (r2t, r2a, r2b), (r3t, r3a, r3b), (r4t, r4a, r4b),
    )
    sw, tw = ws.shape[1], wt.shape[1]
    group = chans // GROUPS
    f = lax.axis_index("frame")
    t = lax.axis_index("tile")
    y, x = f // 2, f % 2
    z, c = t // 2, t % 2
    zh, zl = z // 2, z % 2
    h = heights[0]
    live = iota((1, cells), 1) < h * COLUMNS
    short = h < STRIP_ROWS

    x_peer = (y * 2 + (1 - x), t)
    y_peer = ((1 - y) * 2 + x, t)
    z0_peer = (f, (zh * 2 + (1 - zl)) * 2 + c)
    z1_peer = (f, ((1 - zh) * 2 + zl) * 2 + c)
    c_peer = (f, z * 2 + (1 - c))

    barrier = pltpu.get_barrier_semaphore()
    for d in range(1, tiles):
        pl.semaphore_signal(barrier, inc=1, device_id=(f, (t + d) % tiles), device_id_type=MESH)
    for d in range(1, frames):
        pl.semaphore_signal(barrier, inc=1, device_id=((f + d) % frames, t), device_id_type=MESH)

    eye_ref[...] = jnp.where(iota((chans, chans), 0) == iota((chans, chans), 1), 1.0, 0.0)
    same_ref[...] = jnp.where(
        group_of(chans, group, 0) == group_of(chans, group, 1), 1.0, 0.0
    )

    def row_of(column):
        return jnp.sum(eye_ref[...] * column, axis=0, keepdims=True)

    def column_of(row):
        return jnp.sum(eye_ref[...] * row, axis=1, keepdims=True)

    def group_column(row):
        return jnp.sum(same_ref[...] * row, axis=1, keepdims=True)

    q_own = jnp.where(zh == 0, y, x)
    p_own = jnp.where(zh == 0, x, y)
    slot_own = q_own * 4 + p_own * 2 + zl
    def halves(src, wide):
        w32 = src[...].astype(F32)
        w32 = jnp.concatenate([w32, jnp.zeros((own, wide - w32.shape[1]), F32)], axis=1)
        first, second = w32[:, : wide // 2], w32[:, wide // 2 :]
        return jnp.where(c == 0, first, second), jnp.where(c == 0, second, first)

    kept_t, sent_t = halves(wt, tp)
    kept_s, sent_s = halves(ws, sp)
    kept = (kept_t, kept_s[:, : lanes[1]], kept_s[:, lanes[1] :])
    sent = (sent_t, sent_s[:, : lanes[1]], sent_s[:, lanes[1] :])

    def staged(ref, rows):
        ref[...] = jnp.concatenate(
            [rows, jnp.zeros((ref.shape[0] - own, rows.shape[1]), F32)], axis=0
        ).astype(BF)

    for ref, rows in zip((xs_t, xs_a, xs_b), sent):
        staged(ref, rows)
    masked = jnp.where(live, lat[...].astype(F32), 0.0)
    count_row = jnp.zeros((1, 128), F32) + h.astype(F32) * COLUMNS
    own_rows = [
        row_of(jnp.sum(masked, axis=1, keepdims=True)),
        row_of(jnp.sum(masked * masked, axis=1, keepdims=True)),
        count_row,
    ]
    gain_row = gain[...].reshape(1, chans)
    gain_column = column_of(gain_row)
    shift_column = column_of(shift[...].reshape(1, chans))
    pl.semaphore_wait(barrier, tiles + frames - 2)

    pending = []

    def remote(src, dst, ss, rs, peer):
        copy = pltpu.make_async_remote_copy(
            src_ref=src, dst_ref=dst, send_sem=ss, recv_sem=rs, device_id=peer, device_id_type=MESH
        )
        copy.start()
        pending.append(copy)
        return copy

    def trade(which, kind, src, dst):
        return [
            remote(src, dst, tr_send.at[which, kind], tr_recv.at[which, kind], c_peer)
        ]

    def gather_step(kind, step):
        buf = gathered[kind]
        if step == 0:
            moves = [(0, (c, zh, pl.ds(slot_own, 1)), z1_peer)]
        elif step == 1:
            moves = [
                (1, (c, 0, pl.ds(y * 4 + x * 2 + zl, 1)), z0_peer),
                (2, (c, 1, pl.ds(x * 4 + y * 2 + zl, 1)), z0_peer),
            ]
        elif step == 2:
            moves = [
                (3, (c, 0, pl.ds(y * 4 + x * 2, 2)), x_peer),
                (4, (c, 1, pl.ds(x * 4 + y * 2, 2)), y_peer),
            ]
        elif step == 3:
            moves = [
                (5, (c, 0, pl.ds(y * 4, 4)), y_peer),
                (6, (c, 1, pl.ds(x * 4, 4)), x_peer),
            ]
        else:
            moves = [(7, (c,), c_peer)]
        return [
            remote(buf.at[at], buf.at[at], ag_send.at[kind, i], ag_recv.at[kind, i], peer)
            for i, at, peer in moves
        ]

    def arrived(copies):
        for copy in copies:
            copy.wait_recv()

    def frame_copies(src, prev_dst, next_dst, base):
        up = pltpu.make_async_remote_copy(
            src_ref=src, dst_ref=prev_dst, send_sem=fr_send.at[base], recv_sem=fr_recv.at[base],
            device_id=((f + 1) % frames, t), device_id_type=MESH,
        )
        down = pltpu.make_async_remote_copy(
            src_ref=src, dst_ref=next_dst, send_sem=fr_send.at[base + 1], recv_sem=fr_recv.at[base + 1],
            device_id=((f + frames - 1) % frames, t), device_id_type=MESH,
        )
        return up, down

    def frame_start(pair):
        pl.when(f < frames - 1)(lambda: pair[0].start())
        pl.when(f > 0)(lambda: pair[1].start())

    def frame_arrived(pair):
        pl.when(f > 0)(lambda: pair[0].wait_recv())
        pl.when(f < frames - 1)(lambda: pair[1].wait_recv())

    def frame_sent(pair):
        pl.when(f < frames - 1)(lambda: pair[0].wait_send())
        pl.when(f > 0)(lambda: pair[1].wait_send())

    def strip_copies(which):
        down = pltpu.make_async_remote_copy(
            src_ref=hsend.at[which, 0], dst_ref=hrecv.at[which, 0],
            send_sem=ha_send.at[which, 0], recv_sem=ha_recv.at[which, 0],
            device_id=(f, (t + 1) % tiles), device_id_type=MESH,
        )
        up = pltpu.make_async_remote_copy(
            src_ref=hsend.at[which, 1], dst_ref=hrecv.at[which, 1],
            send_sem=ha_send.at[which, 1], recv_sem=ha_recv.at[which, 1],
            device_id=(f, (t + tiles - 1) % tiles), device_id_type=MESH,
        )
        return down, up

    def strip_start(pair, which, grid):
        half = cells // 2
        hsend[which, 0] = jnp.where(short, grid[:, :half], grid[:, half:]).astype(BF)
        hsend[which, 1] = grid[:, :half].astype(BF)
        pl.when(t < tiles - 1)(lambda: pair[0].start())
        pl.when(t > 0)(lambda: pair[1].start())

    def strip_arrived(pair):
        pl.when(t > 0)(lambda: pair[0].wait_recv())
        pl.when(t < tiles - 1)(lambda: pair[1].wait_recv())

    def strip_sent(pair):
        pl.when(t < tiles - 1)(lambda: pair[0].wait_send())
        pl.when(t > 0)(lambda: pair[1].wait_send())

    def strip_extended(which, grid):
        half = cells // 2
        above = hrecv[which, 0].astype(F32)
        below = hrecv[which, 1].astype(F32)
        return jnp.concatenate(
            [above, grid[:, :half], jnp.where(short, below, grid[:, half:]), below], axis=1
        )

    stride = msg.shape[3] // 3

    def sums_start(which, rows):
        row = jnp.zeros((1, msg.shape[3]), F32)
        for i, part in enumerate(rows):
            at = i * stride
            row_parts = [jnp.zeros((1, at), F32)] if at else []
            row_parts.append(part)
            rest = msg.shape[3] - at - part.shape[1]
            if rest:
                row_parts.append(jnp.zeros((1, rest), F32))
            row = row + jnp.concatenate(row_parts, axis=1)
        msg[which, 0] = row
        tbuf[which, t] = msg[which, 0]
        return [
            remote(
                msg.at[which, 0], tbuf.at[which, t], st_send.at[which, d], st_recv.at[which, d],
                (f, (t + d) % tiles),
            )
            for d in range(1, tiles)
        ]

    def sums_middle(which, copies):
        arrived(copies)
        total = tbuf[which, 0]
        for i in range(1, tiles):
            total = total + tbuf[which, i]
        msg[which, 1] = total
        fbuf[which, f] = total
        return [
            remote(
                msg.at[which, 1], fbuf.at[which, f], st_send.at[which, tiles + d],
                st_recv.at[which, tiles + d], ((f + d) % frames, t),
            )
            for d in range(1, frames)
        ]

    def sums_end(which, copies):
        arrived(copies)
        total = fbuf[which, 0]
        for i in range(1, frames):
            total = total + fbuf[which, i]
        return total

    stat = sums_start(0, own_rows)
    traded = [
        trade(0, kind, src, dst)
        for kind, (src, dst) in enumerate(((xs_t, xr_t), (xs_a, xr_a), (xs_b, xr_b)))
    ]
    og_pair = frame_copies(og, ogf.at[0], ogf.at[1], 0)
    frame_start(og_pair)

    @pl.when(f == 0)
    def _():
        ogf[0] = jnp.zeros_like(ogf[0])

    @pl.when(f == frames - 1)
    def _():
        ogf[1] = jnp.zeros_like(ogf[1])

    @pl.when(t == 0)
    def _():
        hrecv[0, 0] = jnp.zeros_like(hrecv[0, 0])
        hrecv[1, 0] = jnp.zeros_like(hrecv[1, 0])

    @pl.when(t == tiles - 1)
    def _():
        hrecv[0, 1] = jnp.zeros_like(hrecv[0, 1])
        hrecv[1, 1] = jnp.zeros_like(hrecv[1, 1])

    sof[3 * chans :] = jnp.zeros((sof.shape[0] - 3 * chans, cells), BF)
    cols[9 * chans :] = jnp.zeros((cols.shape[0] - 9 * chans, cells), BF)

    chain = [None] * 3
    for kind, ref in enumerate((xr_t, xr_a, xr_b)):
        arrived(traded[kind])
        other = ref[0:own].astype(F32)
        gathered[kind][c, zh, slot_own] = jnp.concatenate(
            [jnp.where(c == 0, kept[kind], other), jnp.where(c == 0, other, kept[kind])], axis=0
        ).astype(BF)
        chain[kind] = gather_step(kind, 0)

    def forth(kind, step):
        arrived(chain[kind])
        if step < 5:
            chain[kind] = gather_step(kind, step)

    forth(0, 1)
    stat = sums_middle(0, stat)
    forth(1, 1)
    forth(2, 1)
    forth(0, 2)
    total = sums_end(0, stat)
    count = total[:, 2 * stride : 2 * stride + 1]
    group_count = count * group
    mean = group_column(total[:, 0:chans]) / group_count
    rstd = lax.rsqrt(
        group_column(total[:, stride : stride + chans]) / group_count - mean * mean + EPSILON
    )
    normed = (lat[...].astype(F32) - mean) * rstd
    pre = gain_column * normed + shift_column
    normed_ref[...] = normed
    pre_ref[...] = pre
    act = jnp.where(live, pre * jax.nn.sigmoid(pre), 0.0).astype(BF).astype(F32)
    act_pair = strip_copies(0)
    strip_start(act_pair, 0, act)
    forth(1, 2)
    forth(0, 3)
    forth(2, 2)
    frame_arrived(og_pair)
    og_here = jnp.where(live, og[...], jnp.zeros((), BF))
    og_next = jnp.where(live, ogf[1], jnp.zeros((), BF))
    og_prev = jnp.where(live, ogf[0], jnp.zeros((), BF))
    forth(1, 3)
    forth(0, 4)
    strip_arrived(act_pair)
    ext[...] = strip_extended(0, act)

    width = ext.shape[1]
    chunk = 64
    col = iota((1, cells), 1) % COLUMNS
    left_ok = col >= 1
    right_ok = col < COLUMNS - 1
    half = cells // 2

    def cut(rolled, b):
        piece = rolled[:, half : half + cells]
        if b < 0:
            piece = jnp.where(left_ok, piece, 0.0)
        if b > 0:
            piece = jnp.where(right_ok, piece, 0.0)
        return piece

    def tap_rows(i, carry):
        r = pl.multiple_of(i * chunk, chunk)
        rows = ext[pl.ds(r, chunk)]
        for k in range(9):
            a, b = k // 3 - 1, k % 3 - 1
            s = a * COLUMNS + b
            rolled = pltpu.roll(rows, (-s) % width, 1) if s else rows
            cols[pl.ds(pl.multiple_of(k * chans + r, 64), chunk)] = cut(rolled, b).astype(BF)
        return carry

    lax.fori_loop(0, 1, tap_rows, 0)
    forth(2, 3)
    lax.fori_loop(1, chans // chunk, tap_rows, 0)

    def slots(fi):
        yi, xi = fi // 2, fi % 2
        return yi * 4 + xi * 2, xi * 4 + yi * 2

    def weight(bufs, fi):
        at = slots(fi)
        sides = []
        for side in range(2):
            for buf in bufs:
                sides.append(
                    jnp.concatenate(
                        [buf[side, zi // 2, at[zi // 2] + zi % 2] for zi in range(4)], axis=0
                    )
                )
        return jnp.concatenate(sides, axis=1)

    def put(bufs, fi, value):
        at = slots(fi)
        lane = 0
        for side in range(2):
            for buf in bufs:
                wide = buf.shape[4]
                for zi in range(4):
                    buf[side, zi // 2, at[zi // 2] + zi % 2] = value[
                        zi * rows_in : (zi + 1) * rows_in, lane : lane + wide
                    ].astype(BF)
                lane += wide

    contract_first = (((0,), (0,)), ((), ()))
    contract_last = (((1,), (1,)), ((), ()))

    forth(0, 5)
    windows = (og_next, og_here, og_prev)
    for fi in range(frames):
        block = weight((g_t,), fi)
        lo, hi = fi * tw, (fi + 1) * tw
        taps = [k for k in range(3) if max(lo, k * chans) < min(hi, (k + 1) * chans)]
        window = jnp.concatenate([windows[k] for k in taps], axis=1)
        part = lax.dot_general(block, window, contract_first, preferred_element_type=F32)
        for i, k in enumerate(taps):
            first, last = max(lo, k * chans), min(hi, (k + 1) * chans)
            zbuf[first:last, 0:cells] = part[first - lo : last - lo, i * cells : (i + 1) * cells]
    gs = zbuf[0:chans, 0:cells] + zbuf[chans : 2 * chans, 0:cells]
    gs = gs + zbuf[2 * chans : 3 * chans, 0:cells]
    gs = jnp.where(live, gs, 0.0).astype(BF).astype(F32)
    gs_ref[...] = gs
    gs_pair = strip_copies(1)
    strip_start(gs_pair, 1, gs)

    def spatial_terms(fi, carry):
        here = gs_ref[...].astype(BF)
        piece = cols[pl.ds(pl.multiple_of(fi * sw, 16), sp)]
        put((p_a, p_b), fi, lax.dot_general(here, piece, contract_last, preferred_element_type=F32))
        return carry

    forth(1, 4)
    lax.fori_loop(0, 2, spatial_terms, 0)
    forth(2, 4)
    lax.fori_loop(2, frames, spatial_terms, 0)

    def reduce_step(kind, step):
        buf = partial[kind]
        into = landing[step][kind]
        if step == 0:
            moves = [(0, (1 - c,), into, c_peer)]
        elif step == 1:
            moves = [
                (1, (c, 0, pl.ds((1 - y) * 4, 4)), into.at[0], y_peer),
                (2, (c, 1, pl.ds((1 - x) * 4, 4)), into.at[1], x_peer),
            ]
        elif step == 2:
            moves = [
                (3, (c, 0, pl.ds(y * 4 + (1 - x) * 2, 2)), into.at[0], x_peer),
                (4, (c, 1, pl.ds(x * 4 + (1 - y) * 2, 2)), into.at[1], y_peer),
            ]
        elif step == 3:
            moves = [
                (5, (c, 0, pl.ds(y * 4 + x * 2 + (1 - zl), 1)), into.at[0], z0_peer),
                (6, (c, 1, pl.ds(x * 4 + y * 2 + (1 - zl), 1)), into.at[1], z0_peer),
            ]
        else:
            q = jnp.where(zh == 0, x, y)
            p = jnp.where(zh == 0, y, x)
            moves = [(7, (c, 1 - zh, pl.ds(q * 4 + p * 2 + zl, 1)), into, z1_peer)]
        return [
            remote(buf.at[at], dst, rs_send.at[kind, i], rs_recv.at[kind, i], peer)
            for i, at, dst, peer in moves
        ]

    def reduce_add(kind, step):
        buf = partial[kind]
        into = landing[step][kind]
        blocks = (8, 4, 2, 1)[step]
        starts = (
            (0, 0),
            (y * 4, x * 4),
            (y * 4 + x * 2, x * 4 + y * 2),
            (y * 4 + x * 2 + zl, x * 4 + y * 2 + zl),
        )[step]
        for hi in range(2):
            def add(i, carry):
                here = buf[c, hi, starts[hi] + i].astype(F32) + into[hi, i].astype(F32)
                buf[c, hi, starts[hi] + i] = here.astype(BF)
                return carry

            lax.fori_loop(0, blocks, add, 0)

    back = [None] * 3

    def reduce_start(kind):
        back[kind] = reduce_step(kind, 0)

    def reduce_on(kind, step):
        arrived(back[kind])
        reduce_add(kind, step - 1)
        back[kind] = reduce_step(kind, step)

    reduce_start(1)
    reduce_start(2)
    strip_arrived(gs_pair)
    ext[...] = strip_extended(1, gs_ref[...])
    forth(1, 5)
    forth(2, 5)
    reduce_on(1, 1)

    acc[...] = jnp.zeros_like(acc)

    def forward(fi, carry):
        piece = cols[pl.ds(pl.multiple_of(fi * sw, 16), sp)]
        acc[...] += jnp.dot(weight((g_a, g_b), fi), piece, preferred_element_type=F32)
        return carry

    lax.fori_loop(0, frames, forward, 0)
    spatial_out = jnp.where(live, acc[...], 0.0).astype(BF)
    for k in range(3):
        sof[k * chans : (k + 1) * chans] = spatial_out

    for fi in range(frames):
        lo, hi = fi * tw, (fi + 1) * tw
        piece = sof[lo : lo + tp]
        value = None
        for k in range(3):
            if max(lo, k * chans) < min(hi, (k + 1) * chans):
                term = lax.dot_general(
                    windows[k], piece, contract_last, preferred_element_type=F32
                )
                if value is None:
                    value = term
                else:
                    value = jnp.where(iota((1, tp), 1) < k * chans - lo, value, term)
        put((p_t,), fi, value)
    reduce_start(0)
    reduce_on(2, 1)

    gs_ext = ext[...].astype(BF)
    for fi in range(frames):
        z_part = lax.dot_general(
            weight((g_a, g_b), fi), gs_ext, contract_first, preferred_element_type=F32
        )
        zbuf[fi * sw : (fi + 1) * sw] = z_part[0:sw]
        if fi == 1:
            reduce_on(1, 2)
            reduce_on(0, 1)
            reduce_on(2, 2)

    def tap_sum(i, carry):
        r = pl.multiple_of(i * chunk, chunk)
        total_rows = jnp.zeros((chunk, cells), F32)
        for k in range(9):
            a, b = k // 3 - 1, k % 3 - 1
            s = a * COLUMNS + b
            rows = zbuf[pl.ds(pl.multiple_of(k * chans + r, 64), chunk)]
            rolled = pltpu.roll(rows, s % width, 1) if s else rows
            total_rows = total_rows + cut(rolled, -b)
        pre_rows = pre_ref[pl.ds(r, chunk)]
        sig = jax.nn.sigmoid(pre_rows)
        gpre_ref[pl.ds(r, chunk)] = jnp.where(
            live, total_rows * sig * (1.0 + pre_rows * (1.0 - sig)), 0.0
        )
        return carry

    reduce_on(0, 2)
    lax.fori_loop(0, 1, tap_sum, 0)
    reduce_on(1, 3)
    reduce_on(2, 3)
    reduce_on(0, 3)
    lax.fori_loop(1, 3, tap_sum, 0)
    reduce_on(1, 4)
    reduce_on(2, 4)
    reduce_on(0, 4)
    lax.fori_loop(3, chans // chunk, tap_sum, 0)
    stat = sums_start(
        1,
        [
            row_of(jnp.sum(gpre_ref[...] * normed_ref[...], axis=1, keepdims=True)),
            row_of(jnp.sum(gpre_ref[...], axis=1, keepdims=True)),
        ],
    )

    def finish(kind, out_stage):
        arrived(back[kind])
        block = partial[kind][c, zh, slot_own].astype(F32) + landing[4][kind][0].astype(F32)
        first, second = block[:own], block[own:]
        staged(out_stage, jnp.where(c == 0, second, first))
        return jnp.where(c == 0, first, second)

    mine, swaps = [None] * 3, [None] * 3
    ends = ((ys_t, yr_t), (ys_a, yr_a), (ys_b, yr_b))
    for kind in (1, 2):
        mine[kind] = finish(kind, ends[kind][0])
        swaps[kind] = trade(1, kind, *ends[kind])
    stat = sums_middle(1, stat)
    mine[0] = finish(0, ends[0][0])
    swaps[0] = trade(1, 0, *ends[0])
    sums = sums_end(1, stat)

    scale = lax.rsqrt(count)
    chan_gain, chan_shift = sums[:, 0:chans], sums[:, stride : stride + chans]
    dgain[...] = scale * chan_gain
    dshift[...] = scale * chan_shift
    shift_sum = group_column(gain_row * chan_shift) / group_count
    gain_sum = group_column(gain_row * chan_gain) / group_count
    result = og[...].astype(F32) + rstd * (
        gain_column * gpre_ref[...] - shift_sum - normed_ref[...] * gain_sum
    )
    gi[...] = jnp.where(live, result, 0.0).astype(BF)

    for kind in (1, 2, 0):
        arrived(swaps[kind])
    theirs = [pair[1][0:own].astype(F32) for pair in ends]
    side_s = jnp.concatenate(mine[1:], axis=1), jnp.concatenate(theirs[1:], axis=1)
    for out, (a, b), wide in ((dws, side_s, sw), (dwt, (mine[0], theirs[0]), tw)):
        whole = jnp.concatenate([jnp.where(c == 0, a, b), jnp.where(c == 0, b, a)], axis=1)
        out[...] = scale * whole[:, 0:wide]

    for copy in pending:
        copy.wait_send()
    frame_sent(og_pair)
    for pair in (act_pair, gs_pair):
        strip_sent(pair)


def hand_over(*refs):
    for source, target in zip(refs[:5], refs[5:]):
        target[...] = source[...].reshape(target.shape)


def fused(latents, out_grad, w_spatial, w_temporal, norm_gain, norm_shift, heights):
    chans, cells = latents.shape[1:]
    own, sw = w_spatial.shape
    tw = w_temporal.shape[1]
    pad = -(-own // 16) * 16
    th = -(-tw // 256) * 128
    sh = -(-sw // 256) * 128
    kinds = (th, sh - 128, 128)
    sp, tp = 2 * sh, 2 * th
    wide = -(-chans // 128) * 128

    scratch = (
        [pltpu.VMEM((2, 2, 8, 2 * own, kind), BF) for _ in range(2) for kind in kinds]
        + [
            pltpu.VMEM(lead + (2 * own, kind), BF)
            for lead in ((2, 8), (2, 4), (2, 2), (2, 1), (1,))
            for kind in kinds
        ]
        + [pltpu.VMEM((pad, kind), BF) for _ in range(4) for kind in kinds]
        + [
            pltpu.VMEM((2, chans, cells), BF),
            pltpu.VMEM((3 * chans + tp - tw, cells), BF),
            pltpu.VMEM((2, 2, chans, cells // 2), BF),
            pltpu.VMEM((2, 2, chans, cells // 2), BF),
            pltpu.VMEM((chans, 2 * cells), F32),
            pltpu.VMEM((9 * chans + sp - sw, cells), BF),
            pltpu.VMEM((9 * chans, 2 * cells), F32),
            pltpu.VMEM((chans, cells), F32),
        ]
        + [pltpu.VMEM((chans, cells), F32)] * 4
        + [
            pltpu.VMEM((2, 2, 1, 3 * wide), F32),
            pltpu.VMEM((2, 8, 1, 3 * wide), F32),
            pltpu.VMEM((2, 4, 1, 3 * wide), F32),
            pltpu.VMEM((chans, chans), F32),
            pltpu.VMEM((chans, chans), F32),
        ]
        + [pltpu.SemaphoreType.DMA((3, 8))] * 4
        + [pltpu.SemaphoreType.DMA((2,))] * 2
        + [pltpu.SemaphoreType.DMA((2, 2))] * 2
        + [pltpu.SemaphoreType.DMA((2, 12))] * 2
        + [pltpu.SemaphoreType.DMA((2, 3))] * 2
    )
    vmem = pl.BlockSpec(memory_space=pltpu.VMEM)
    outs = pl.pallas_call(
        whole_kernel,
        out_shape=(
            jax.ShapeDtypeStruct((chans, cells), BF),
            jax.ShapeDtypeStruct((own, sw), F32),
            jax.ShapeDtypeStruct((own, tw), F32),
            jax.ShapeDtypeStruct((1, chans), F32),
            jax.ShapeDtypeStruct((1, chans), F32),
        ),
        in_specs=[vmem] * 6 + [pl.BlockSpec(memory_space=pltpu.SMEM)],
        out_specs=(vmem,) * 5,
        scratch_shapes=scratch,
        compiler_params=pltpu.CompilerParams(
            collective_id=0, has_side_effects=True, vmem_limit_bytes=56 * 1024 * 1024
        ),
    )(
        latents[0], out_grad[0], w_spatial, w_temporal, norm_gain, norm_shift, heights
    )
    shapes = [outs[0].shape, outs[1].shape, outs[2].shape, (chans,), (chans,)]
    results = pl.pallas_call(
        hand_over,
        out_shape=tuple(
            jax.ShapeDtypeStruct(shape, out.dtype) for shape, out in zip(shapes, outs)
        ),
        in_specs=[vmem] * 5,
        out_specs=(vmem,) * 5,
    )(*outs)
    return (results[0][None],) + tuple(results[1:])


def solution(mesh):
    in_specs = (
        P("frame", None, "tile"),
        P("frame", None, "tile"),
        P("tile", "frame"),
        P("tile", "frame"),
        P(),
        P(),
        P("tile"),
    )
    out_specs = (P("frame", None, "tile"), P("tile", "frame"), P("tile", "frame"), P(), P())
    fits = mesh.shape["frame"] == 4 and mesh.shape["tile"] == 8
    return jax.shard_map(
        fused if fits else local, mesh=mesh, in_specs=in_specs, out_specs=out_specs, check_vma=False
    )
```

```python
import jax
import jax.numpy as jnp
from jax import lax
from jax.experimental import pallas as pl
from jax.experimental.pallas import tpu as pltpu
from jax.sharding import PartitionSpec as P

GROUPS = 32
COLUMNS = 16
STRIP_ROWS = 16


EPSILON = 1e-05


def from_behind(shard, axis, by):
    peers = lax.axis_size(axis)
    pairs = [(i, i + by) for i in range(peers) if 0 <= i + by < peers]
    return lax.ppermute(shard, axis, pairs)


def padded_2(cells, sides, width):
    for axis, dim in sides:
        count = lax.axis_size(axis)
        ends = count - 1
        head = lax.slice_in_dim(cells, 0, width, axis=dim)
        tail = lax.slice_in_dim(cells, cells.shape[dim] - width, cells.shape[dim], axis=dim)
        cells = jnp.concatenate(
            [
                lax.ppermute(tail, axis, [(i, (i + 1) % count) for i in range(ends)]),
                cells,
                lax.ppermute(head, axis, [((i + 1) % count, i) for i in range(ends)]),
            ],
            axis=dim,
        )
    return cells


def flip_taps(weight, tap_count):
    outputs = weight.shape[0]
    return jnp.transpose(weight.reshape(outputs, tap_count, -1)[:, ::-1, :], (2, 1, 0)).reshape(
        -1, tap_count * outputs
    )


def padded_rows(row_grid, above_row, below_row, height):
    channel_count = row_grid.shape[0]
    padded = jnp.zeros((channel_count, STRIP_ROWS + 2, COLUMNS + 2), row_grid.dtype)
    padded = padded.at[:, 1 : STRIP_ROWS + 1, 1 : COLUMNS + 1].set(row_grid)
    padded = padded.at[:, 0, 1 : COLUMNS + 1].set(above_row)
    below_block = jnp.pad(below_row, ((0, 0), (1, 1)))[:, None, :]
    return lax.dynamic_update_slice(padded, below_block, (jnp.int32(0), height + 1, jnp.int32(0)))


def tap_columns(padded, row_count):
    pieces = [
        padded[:, row_step : row_step + row_count, col_step : col_step + COLUMNS]
        for row_step in range(3)
        for col_step in range(3)
    ]
    return jnp.stack(pieces, axis=0).reshape(9 * padded.shape[0], row_count * COLUMNS)


def local(latents, out_grad, w_spatial, w_temporal, norm_gain, norm_shift, heights):
    channel_count = latents.shape[1]
    cell_count = latents.shape[2]
    group_size = channel_count // GROUPS
    height = heights[0]
    slot_row = jnp.arange(cell_count, dtype=jnp.int32) // COLUMNS
    live_cells = slot_row < height
    live_float = live_cells.astype(jnp.float32)
    contract_last = (((1,), (1,)), ((), ()))
    part_spatial_w, part_temporal_w = (
        lax.all_gather(w_spatial, "frame", axis=1, tiled=True),
        lax.all_gather(w_temporal, "frame", axis=1, tiled=True),
    )
    spatial_full, temporal_full = (
        lax.all_gather(part_spatial_w, "tile", axis=0, tiled=True),
        lax.all_gather(part_temporal_w, "tile", axis=0, tiled=True),
    )
    latent_full = latents[0].astype(jnp.float32)
    masked = latent_full * live_float[None, :]
    group_sum = masked.reshape(GROUPS, group_size, cell_count).sum(axis=(1, 2))
    group_square = (masked * latent_full).reshape(GROUPS, group_size, cell_count).sum(axis=(1, 2))
    own_count = height.astype(jnp.float32) * COLUMNS
    total_sum, total_square, position_count = lax.psum(
        (group_sum, group_square, own_count), ("frame", "tile")
    )
    group_count = position_count * group_size
    group_mean = total_sum / group_count
    group_rstd = lax.rsqrt(total_square / group_count - group_mean * group_mean + EPSILON)
    mean_column = jnp.repeat(group_mean, group_size)[:, None]
    rstd_column = jnp.repeat(group_rstd, group_size)[:, None]
    gain_column = norm_gain[:, None]
    normed = (latent_full - mean_column) * rstd_column
    pre_act = gain_column * normed + norm_shift[:, None]
    activated = jnp.where(live_cells[None, :], jax.nn.silu(pre_act), 0.0).astype(jnp.bfloat16)
    act_grid = activated.reshape(channel_count, STRIP_ROWS, COLUMNS)
    last_live = lax.dynamic_slice_in_dim(act_grid, height - 1, 1, 1)[:, 0, :]
    from_above = from_behind(last_live, "tile", 1)
    from_below = from_behind(act_grid[:, 0, :], "tile", -1)
    act_padded = padded_rows(act_grid, from_above, from_below, height)
    act_columns = tap_columns(act_padded, STRIP_ROWS)
    spatial_raw = jnp.dot(spatial_full, act_columns, preferred_element_type=jnp.float32)
    spatial_out = jnp.where(live_cells[None, :], spatial_raw, 0.0).astype(jnp.bfloat16)
    spatial_frames = padded_2(spatial_out[None], (("frame", 0),), 1)
    grad_here = jnp.where(live_cells[None, :], out_grad[0], jnp.zeros((), jnp.bfloat16))
    grad_frames = padded_2(grad_here[None], (("frame", 0),), 1)
    part_temporal = lax.dot_general(
        grad_here,
        spatial_frames.reshape(3 * channel_count, cell_count),
        contract_last,
        preferred_element_type=jnp.float32,
    )
    grad_spat = jnp.dot(
        flip_taps(temporal_full, 3),
        grad_frames.reshape(3 * channel_count, cell_count),
        preferred_element_type=jnp.float32,
    )
    grad_spat = jnp.where(live_cells[None, :], grad_spat, 0.0).astype(jnp.bfloat16)
    spat_grid = grad_spat.reshape(channel_count, STRIP_ROWS, COLUMNS)
    grad_last = lax.dynamic_slice_in_dim(spat_grid, height - 1, 1, 1)[:, 0, :]
    grad_above = from_behind(grad_last, "tile", 1)
    grad_below = from_behind(spat_grid[:, 0, :], "tile", -1)
    grad_padded = padded_rows(spat_grid, grad_above, grad_below, height)
    spatial_flip = flip_taps(spatial_full, 9)
    grad_act = jnp.dot(
        spatial_flip, tap_columns(grad_padded, STRIP_ROWS), preferred_element_type=jnp.float32
    )
    part_spatial = lax.dot_general(
        grad_spat, act_columns, contract_last, preferred_element_type=jnp.float32
    )
    sigmoid_act = jax.nn.sigmoid(pre_act)
    grad_pre = jnp.where(
        live_cells[None, :], grad_act * sigmoid_act * (1.0 + pre_act * (1.0 - sigmoid_act)), 0.0
    )
    chan_gain, chan_shift = lax.psum(
        (jnp.sum(grad_pre * normed, axis=1), jnp.sum(grad_pre, axis=1)), ("frame", "tile")
    )
    shift_sum = (norm_gain * chan_shift).reshape(GROUPS, group_size).sum(1) / group_count
    gain_sum = (norm_gain * chan_gain).reshape(GROUPS, group_size).sum(1) / group_count
    result = grad_here.astype(jnp.float32) + rstd_column * (
        gain_column * grad_pre
        - jnp.repeat(shift_sum, group_size)[:, None]
        - normed * jnp.repeat(gain_sum, group_size)[:, None]
    )
    grad_input = jnp.where(live_cells[None, :], result, 0.0).astype(jnp.bfloat16)[None]
    tile_spatial, tile_temporal = (
        lax.psum_scatter(
            part_spatial.astype(jnp.bfloat16), "tile", scatter_dimension=0, tiled=True
        ).astype(jnp.float32),
        lax.psum_scatter(
            part_temporal.astype(jnp.bfloat16), "tile", scatter_dimension=0, tiled=True
        ).astype(jnp.float32),
    )
    grad_spatial, grad_temporal = (
        lax.psum_scatter(
            tile_spatial.astype(jnp.bfloat16), "frame", scatter_dimension=1, tiled=True
        ).astype(jnp.float32),
        lax.psum_scatter(
            tile_temporal.astype(jnp.bfloat16), "frame", scatter_dimension=1, tiled=True
        ).astype(jnp.float32),
    )
    grad_scale = lax.rsqrt(position_count)
    return (
        grad_input,
        grad_scale * grad_spatial,
        grad_scale * grad_temporal,
        grad_scale * chan_gain,
        grad_scale * chan_shift,
    )


MESH = pl.DeviceIdType.MESH
BF = jnp.bfloat16
F32 = jnp.float32


def iota(shape, dim):
    return lax.broadcasted_iota(jnp.int32, shape, dim)


def group_of(n, size, dim):
    factor = (1 << 11) // size + 1
    return lax.shift_right_logical(iota((n, n), dim) * factor, 11)


def whole_kernel(
    lat, og, ws, wt, gain, shift, heights,
    gi, dws, dwt, dgain, dshift,
    g_t, g_a, g_b, p_t, p_a, p_b,
    r0t, r0a, r0b, r1t, r1a, r1b, r2t, r2a, r2b, r3t, r3a, r3b, r4t, r4a, r4b,
    xs_t, xs_a, xs_b, xr_t, xr_a, xr_b, ys_t, ys_a, ys_b, yr_t, yr_a, yr_b,
    ogf, sof, hsend, hrecv, ext, cols, zbuf, acc, normed_ref, pre_ref, gs_ref, gpre_ref,
    msg, tbuf, fbuf, eye_ref, same_ref,
    ag_send, ag_recv, rs_send, rs_recv, fr_send, fr_recv, ha_send, ha_recv, st_send, st_recv, tr_send, tr_recv,
):
    frames, tiles = 4, 8
    chans, cells = lat.shape
    own = ws.shape[0]
    lanes = tuple(buf.shape[4] for buf in (g_t, g_a, g_b))
    rows_in = 2 * own
    sp = 2 * (lanes[1] + lanes[2])
    tp = 2 * lanes[0]
    gathered, partial = (g_t, g_a, g_b), (p_t, p_a, p_b)
    landing = (
        (r0t, r0a, r0b), (r1t, r1a, r1b), (r2t, r2a, r2b), (r3t, r3a, r3b), (r4t, r4a, r4b),
    )
    sw, tw = ws.shape[1], wt.shape[1]
    group = chans // GROUPS
    f = lax.axis_index("frame")
    t = lax.axis_index("tile")
    y, x = f // 2, f % 2
    z, c = t // 2, t % 2
    zh, zl = z // 2, z % 2
    h = heights[0]
    live = iota((1, cells), 1) < h * COLUMNS
    short = h < STRIP_ROWS

    x_peer = (y * 2 + (1 - x), t)
    y_peer = ((1 - y) * 2 + x, t)
    z0_peer = (f, (zh * 2 + (1 - zl)) * 2 + c)
    z1_peer = (f, ((1 - zh) * 2 + zl) * 2 + c)
    c_peer = (f, z * 2 + (1 - c))

    barrier = pltpu.get_barrier_semaphore()
    for d in range(1, tiles):
        pl.semaphore_signal(barrier, inc=1, device_id=(f, (t + d) % tiles), device_id_type=MESH)
    for d in range(1, frames):
        pl.semaphore_signal(barrier, inc=1, device_id=((f + d) % frames, t), device_id_type=MESH)

    eye_ref[...] = jnp.where(iota((chans, chans), 0) == iota((chans, chans), 1), 1.0, 0.0)
    same_ref[...] = jnp.where(
        group_of(chans, group, 0) == group_of(chans, group, 1), 1.0, 0.0
    )

    def row_of(column):
        return jnp.sum(eye_ref[...] * column, axis=0, keepdims=True)

    def column_of(row):
        return jnp.sum(eye_ref[...] * row, axis=1, keepdims=True)

    def group_column(row):
        return jnp.sum(same_ref[...] * row, axis=1, keepdims=True)

    q_own = jnp.where(zh == 0, y, x)
    p_own = jnp.where(zh == 0, x, y)
    slot_own = q_own * 4 + p_own * 2 + zl
    def halves(src, wide):
        w32 = src[...].astype(F32)
        w32 = jnp.concatenate([w32, jnp.zeros((own, wide - w32.shape[1]), F32)], axis=1)
        first, second = w32[:, : wide // 2], w32[:, wide // 2 :]
        return jnp.where(c == 0, first, second), jnp.where(c == 0, second, first)

    kept_t, sent_t = halves(wt, tp)
    kept_s, sent_s = halves(ws, sp)
    kept = (kept_t, kept_s[:, : lanes[1]], kept_s[:, lanes[1] :])
    sent = (sent_t, sent_s[:, : lanes[1]], sent_s[:, lanes[1] :])

    def staged(ref, rows):
        ref[...] = jnp.concatenate(
            [rows, jnp.zeros((ref.shape[0] - own, rows.shape[1]), F32)], axis=0
        ).astype(BF)

    for ref, rows in zip((xs_t, xs_a, xs_b), sent):
        staged(ref, rows)
    masked = jnp.where(live, lat[...].astype(F32), 0.0)
    count_row = jnp.zeros((1, 128), F32) + h.astype(F32) * COLUMNS
    own_rows = [
        row_of(jnp.sum(masked, axis=1, keepdims=True)),
        row_of(jnp.sum(masked * masked, axis=1, keepdims=True)),
        count_row,
    ]
    gain_row = gain[...].reshape(1, chans)
    gain_column = column_of(gain_row)
    shift_column = column_of(shift[...].reshape(1, chans))
    pl.semaphore_wait(barrier, tiles + frames - 2)

    pending = []

    def remote(src, dst, ss, rs, peer):
        copy = pltpu.make_async_remote_copy(
            src_ref=src, dst_ref=dst, send_sem=ss, recv_sem=rs, device_id=peer, device_id_type=MESH
        )
        copy.start()
        pending.append(copy)
        return copy

    def trade(which, kind, src, dst):
        return [
            remote(src, dst, tr_send.at[which, kind], tr_recv.at[which, kind], c_peer)
        ]

    def gather_step(kind, step):
        buf = gathered[kind]
        if step == 0:
            moves = [(0, (c, zh, pl.ds(slot_own, 1)), z1_peer)]
        elif step == 1:
            moves = [
                (1, (c, 0, pl.ds(y * 4 + x * 2 + zl, 1)), z0_peer),
                (2, (c, 1, pl.ds(x * 4 + y * 2 + zl, 1)), z0_peer),
            ]
        elif step == 2:
            moves = [
                (3, (c, 0, pl.ds(y * 4 + x * 2, 2)), x_peer),
                (4, (c, 1, pl.ds(x * 4 + y * 2, 2)), y_peer),
            ]
        elif step == 3:
            moves = [
                (5, (c, 0, pl.ds(y * 4, 4)), y_peer),
                (6, (c, 1, pl.ds(x * 4, 4)), x_peer),
            ]
        else:
            moves = [(7, (c,), c_peer)]
        return [
            remote(buf.at[at], buf.at[at], ag_send.at[kind, i], ag_recv.at[kind, i], peer)
            for i, at, peer in moves
        ]

    def arrived(copies):
        for copy in copies:
            copy.wait_recv()

    def frame_copies(src, prev_dst, next_dst, base):
        up = pltpu.make_async_remote_copy(
            src_ref=src, dst_ref=prev_dst, send_sem=fr_send.at[base], recv_sem=fr_recv.at[base],
            device_id=((f + 1) % frames, t), device_id_type=MESH,
        )
        down = pltpu.make_async_remote_copy(
            src_ref=src, dst_ref=next_dst, send_sem=fr_send.at[base + 1], recv_sem=fr_recv.at[base + 1],
            device_id=((f + frames - 1) % frames, t), device_id_type=MESH,
        )
        return up, down

    def frame_start(pair):
        pl.when(f < frames - 1)(lambda: pair[0].start())
        pl.when(f > 0)(lambda: pair[1].start())

    def frame_arrived(pair):
        pl.when(f > 0)(lambda: pair[0].wait_recv())
        pl.when(f < frames - 1)(lambda: pair[1].wait_recv())

    def frame_sent(pair):
        pl.when(f < frames - 1)(lambda: pair[0].wait_send())
        pl.when(f > 0)(lambda: pair[1].wait_send())

    def strip_copies(which):
        down = pltpu.make_async_remote_copy(
            src_ref=hsend.at[which, 0], dst_ref=hrecv.at[which, 0],
            send_sem=ha_send.at[which, 0], recv_sem=ha_recv.at[which, 0],
            device_id=(f, (t + 1) % tiles), device_id_type=MESH,
        )
        up = pltpu.make_async_remote_copy(
            src_ref=hsend.at[which, 1], dst_ref=hrecv.at[which, 1],
            send_sem=ha_send.at[which, 1], recv_sem=ha_recv.at[which, 1],
            device_id=(f, (t + tiles - 1) % tiles), device_id_type=MESH,
        )
        return down, up

    def strip_start(pair, which, grid):
        half = cells // 2
        hsend[which, 0] = jnp.where(short, grid[:, :half], grid[:, half:]).astype(BF)
        hsend[which, 1] = grid[:, :half].astype(BF)
        pl.when(t < tiles - 1)(lambda: pair[0].start())
        pl.when(t > 0)(lambda: pair[1].start())

    def strip_arrived(pair):
        pl.when(t > 0)(lambda: pair[0].wait_recv())
        pl.when(t < tiles - 1)(lambda: pair[1].wait_recv())

    def strip_sent(pair):
        pl.when(t < tiles - 1)(lambda: pair[0].wait_send())
        pl.when(t > 0)(lambda: pair[1].wait_send())

    def strip_extended(which, grid):
        half = cells // 2
        above = hrecv[which, 0].astype(F32)
        below = hrecv[which, 1].astype(F32)
        return jnp.concatenate(
            [above, grid[:, :half], jnp.where(short, below, grid[:, half:]), below], axis=1
        )

    stride = msg.shape[3] // 3

    def sums_start(which, rows):
        row = jnp.zeros((1, msg.shape[3]), F32)
        for i, part in enumerate(rows):
            at = i * stride
            row_parts = [jnp.zeros((1, at), F32)] if at else []
            row_parts.append(part)
            rest = msg.shape[3] - at - part.shape[1]
            if rest:
                row_parts.append(jnp.zeros((1, rest), F32))
            row = row + jnp.concatenate(row_parts, axis=1)
        msg[which, 0] = row
        tbuf[which, t] = msg[which, 0]
        return [
            remote(
                msg.at[which, 0], tbuf.at[which, t], st_send.at[which, d], st_recv.at[which, d],
                (f, (t + d) % tiles),
            )
            for d in range(1, tiles)
        ]

    def sums_middle(which, copies):
        arrived(copies)
        total = tbuf[which, 0]
        for i in range(1, tiles):
            total = total + tbuf[which, i]
        msg[which, 1] = total
        fbuf[which, f] = total
        return [
            remote(
                msg.at[which, 1], fbuf.at[which, f], st_send.at[which, tiles + d],
                st_recv.at[which, tiles + d], ((f + d) % frames, t),
            )
            for d in range(1, frames)
        ]

    def sums_end(which, copies):
        arrived(copies)
        total = fbuf[which, 0]
        for i in range(1, frames):
            total = total + fbuf[which, i]
        return total

    stat = sums_start(0, own_rows)
    traded = [
        trade(0, kind, src, dst)
        for kind, (src, dst) in enumerate(((xs_t, xr_t), (xs_a, xr_a), (xs_b, xr_b)))
    ]
    og_pair = frame_copies(og, ogf.at[0], ogf.at[1], 0)
    frame_start(og_pair)

    @pl.when(f == 0)
    def _():
        ogf[0] = jnp.zeros_like(ogf[0])

    @pl.when(f == frames - 1)
    def _():
        ogf[1] = jnp.zeros_like(ogf[1])

    @pl.when(t == 0)
    def _():
        hrecv[0, 0] = jnp.zeros_like(hrecv[0, 0])
        hrecv[1, 0] = jnp.zeros_like(hrecv[1, 0])

    @pl.when(t == tiles - 1)
    def _():
        hrecv[0, 1] = jnp.zeros_like(hrecv[0, 1])
        hrecv[1, 1] = jnp.zeros_like(hrecv[1, 1])

    sof[3 * chans :] = jnp.zeros((sof.shape[0] - 3 * chans, cells), BF)
    cols[9 * chans :] = jnp.zeros((cols.shape[0] - 9 * chans, cells), BF)

    chain = [None] * 3
    for kind, ref in enumerate((xr_t, xr_a, xr_b)):
        arrived(traded[kind])
        other = ref[0:own].astype(F32)
        gathered[kind][c, zh, slot_own] = jnp.concatenate(
            [jnp.where(c == 0, kept[kind], other), jnp.where(c == 0, other, kept[kind])], axis=0
        ).astype(BF)
        chain[kind] = gather_step(kind, 0)

    def forth(kind, step):
        arrived(chain[kind])
        if step < 5:
            chain[kind] = gather_step(kind, step)

    forth(0, 1)
    stat = sums_middle(0, stat)
    forth(1, 1)
    forth(2, 1)
    forth(0, 2)
    total = sums_end(0, stat)
    count = total[:, 2 * stride : 2 * stride + 1]
    group_count = count * group
    mean = group_column(total[:, 0:chans]) / group_count
    rstd = lax.rsqrt(
        group_column(total[:, stride : stride + chans]) / group_count - mean * mean + EPSILON
    )
    normed = (lat[...].astype(F32) - mean) * rstd
    pre = gain_column * normed + shift_column
    normed_ref[...] = normed
    pre_ref[...] = pre
    act = jnp.where(live, pre * jax.nn.sigmoid(pre), 0.0).astype(BF).astype(F32)
    act_pair = strip_copies(0)
    strip_start(act_pair, 0, act)
    forth(1, 2)
    forth(0, 3)
    forth(2, 2)
    forth(1, 3)
    forth(0, 4)
    strip_arrived(act_pair)
    ext[...] = strip_extended(0, act)

    width = ext.shape[1]
    chunk = 64
    col = iota((1, cells), 1) % COLUMNS
    left_ok = col >= 1
    right_ok = col < COLUMNS - 1
    half = cells // 2

    def cut(rolled, b):
        piece = rolled[:, half : half + cells]
        if b < 0:
            piece = jnp.where(left_ok, piece, 0.0)
        if b > 0:
            piece = jnp.where(right_ok, piece, 0.0)
        return piece

    def tap_rows(i, carry):
        r = pl.multiple_of(i * chunk, chunk)
        rows = ext[pl.ds(r, chunk)]
        for k in range(9):
            a, b = k // 3 - 1, k % 3 - 1
            s = a * COLUMNS + b
            rolled = pltpu.roll(rows, (-s) % width, 1) if s else rows
            cols[pl.ds(pl.multiple_of(k * chans + r, 64), chunk)] = cut(rolled, b).astype(BF)
        return carry

    lax.fori_loop(0, 1, tap_rows, 0)
    forth(2, 3)
    lax.fori_loop(1, chans // chunk, tap_rows, 0)

    def slots(fi):
        yi, xi = fi // 2, fi % 2
        return yi * 4 + xi * 2, xi * 4 + yi * 2

    def weight(bufs, fi):
        at = slots(fi)
        sides = []
        for side in range(2):
            for buf in bufs:
                sides.append(
                    jnp.concatenate(
                        [buf[side, zi // 2, at[zi // 2] + zi % 2] for zi in range(4)], axis=0
                    )
                )
        return jnp.concatenate(sides, axis=1)

    def put(bufs, fi, value):
        at = slots(fi)
        lane = 0
        for side in range(2):
            for buf in bufs:
                wide = buf.shape[4]
                for zi in range(4):
                    buf[side, zi // 2, at[zi // 2] + zi % 2] = value[
                        zi * rows_in : (zi + 1) * rows_in, lane : lane + wide
                    ].astype(BF)
                lane += wide

    contract_first = (((0,), (0,)), ((), ()))
    contract_last = (((1,), (1,)), ((), ()))

    frame_arrived(og_pair)
    og_here = jnp.where(live, og[...], jnp.zeros((), BF))
    og_next = jnp.where(live, ogf[1], jnp.zeros((), BF))
    og_prev = jnp.where(live, ogf[0], jnp.zeros((), BF))
    forth(0, 5)
    windows = (og_next, og_here, og_prev)
    for fi in range(frames):
        block = weight((g_t,), fi)
        lo, hi = fi * tw, (fi + 1) * tw
        taps = [k for k in range(3) if max(lo, k * chans) < min(hi, (k + 1) * chans)]
        window = jnp.concatenate([windows[k] for k in taps], axis=1)
        part = lax.dot_general(block, window, contract_first, preferred_element_type=F32)
        for i, k in enumerate(taps):
            first, last = max(lo, k * chans), min(hi, (k + 1) * chans)
            zbuf[first:last, 0:cells] = part[first - lo : last - lo, i * cells : (i + 1) * cells]
    gs = zbuf[0:chans, 0:cells] + zbuf[chans : 2 * chans, 0:cells]
    gs = gs + zbuf[2 * chans : 3 * chans, 0:cells]
    gs = jnp.where(live, gs, 0.0).astype(BF).astype(F32)
    gs_ref[...] = gs
    gs_pair = strip_copies(1)
    strip_start(gs_pair, 1, gs)

    def spatial_terms(fi, carry):
        here = gs_ref[...].astype(BF)
        piece = cols[pl.ds(pl.multiple_of(fi * sw, 16), sp)]
        put((p_a, p_b), fi, lax.dot_general(here, piece, contract_last, preferred_element_type=F32))
        return carry

    forth(1, 4)
    lax.fori_loop(0, 2, spatial_terms, 0)
    forth(2, 4)
    lax.fori_loop(2, frames, spatial_terms, 0)

    def reduce_step(kind, step):
        buf = partial[kind]
        into = landing[step][kind]
        if step == 0:
            moves = [(0, (1 - c,), into, c_peer)]
        elif step == 1:
            moves = [
                (1, (c, 0, pl.ds((1 - y) * 4, 4)), into.at[0], y_peer),
                (2, (c, 1, pl.ds((1 - x) * 4, 4)), into.at[1], x_peer),
            ]
        elif step == 2:
            moves = [
                (3, (c, 0, pl.ds(y * 4 + (1 - x) * 2, 2)), into.at[0], x_peer),
                (4, (c, 1, pl.ds(x * 4 + (1 - y) * 2, 2)), into.at[1], y_peer),
            ]
        elif step == 3:
            moves = [
                (5, (c, 0, pl.ds(y * 4 + x * 2 + (1 - zl), 1)), into.at[0], z0_peer),
                (6, (c, 1, pl.ds(x * 4 + y * 2 + (1 - zl), 1)), into.at[1], z0_peer),
            ]
        else:
            q = jnp.where(zh == 0, x, y)
            p = jnp.where(zh == 0, y, x)
            moves = [(7, (c, 1 - zh, pl.ds(q * 4 + p * 2 + zl, 1)), into, z1_peer)]
        return [
            remote(buf.at[at], dst, rs_send.at[kind, i], rs_recv.at[kind, i], peer)
            for i, at, dst, peer in moves
        ]

    def reduce_add(kind, step):
        buf = partial[kind]
        into = landing[step][kind]
        blocks = (8, 4, 2, 1)[step]
        starts = (
            (0, 0),
            (y * 4, x * 4),
            (y * 4 + x * 2, x * 4 + y * 2),
            (y * 4 + x * 2 + zl, x * 4 + y * 2 + zl),
        )[step]
        for hi in range(2):
            def add(i, carry):
                here = buf[c, hi, starts[hi] + i].astype(F32) + into[hi, i].astype(F32)
                buf[c, hi, starts[hi] + i] = here.astype(BF)
                return carry

            lax.fori_loop(0, blocks, add, 0)

    back = [None] * 3

    def reduce_start(kind):
        back[kind] = reduce_step(kind, 0)

    def reduce_on(kind, step):
        arrived(back[kind])
        reduce_add(kind, step - 1)
        back[kind] = reduce_step(kind, step)

    reduce_start(1)
    reduce_start(2)
    strip_arrived(gs_pair)
    ext[...] = strip_extended(1, gs_ref[...])
    forth(1, 5)
    forth(2, 5)
    reduce_on(1, 1)

    acc[...] = jnp.zeros_like(acc)

    def forward(fi, carry):
        piece = cols[pl.ds(pl.multiple_of(fi * sw, 16), sp)]
        acc[...] += jnp.dot(weight((g_a, g_b), fi), piece, preferred_element_type=F32)
        return carry

    lax.fori_loop(0, frames, forward, 0)
    spatial_out = jnp.where(live, acc[...], 0.0).astype(BF)
    for k in range(3):
        sof[k * chans : (k + 1) * chans] = spatial_out

    for fi in range(frames):
        lo, hi = fi * tw, (fi + 1) * tw
        piece = sof[lo : lo + tp]
        value = None
        for k in range(3):
            if max(lo, k * chans) < min(hi, (k + 1) * chans):
                term = lax.dot_general(
                    windows[k], piece, contract_last, preferred_element_type=F32
                )
                if value is None:
                    value = term
                else:
                    value = jnp.where(iota((1, tp), 1) < k * chans - lo, value, term)
        put((p_t,), fi, value)
    reduce_start(0)
    reduce_on(2, 1)

    gs_ext = ext[...].astype(BF)
    for fi in range(frames):
        z_part = lax.dot_general(
            weight((g_a, g_b), fi), gs_ext, contract_first, preferred_element_type=F32
        )
        zbuf[fi * sw : (fi + 1) * sw] = z_part[0:sw]
        if fi == 1:
            reduce_on(1, 2)
            reduce_on(0, 1)
            reduce_on(2, 2)

    def tap_sum(i, carry):
        r = pl.multiple_of(i * chunk, chunk)
        total_rows = jnp.zeros((chunk, cells), F32)
        for k in range(9):
            a, b = k // 3 - 1, k % 3 - 1
            s = a * COLUMNS + b
            rows = zbuf[pl.ds(pl.multiple_of(k * chans + r, 64), chunk)]
            rolled = pltpu.roll(rows, s % width, 1) if s else rows
            total_rows = total_rows + cut(rolled, -b)
        pre_rows = pre_ref[pl.ds(r, chunk)]
        sig = jax.nn.sigmoid(pre_rows)
        gpre_ref[pl.ds(r, chunk)] = jnp.where(
            live, total_rows * sig * (1.0 + pre_rows * (1.0 - sig)), 0.0
        )
        return carry

    reduce_on(0, 2)
    lax.fori_loop(0, 1, tap_sum, 0)
    reduce_on(1, 3)
    reduce_on(2, 3)
    reduce_on(0, 3)
    lax.fori_loop(1, 3, tap_sum, 0)
    reduce_on(1, 4)
    reduce_on(2, 4)
    reduce_on(0, 4)
    lax.fori_loop(3, chans // chunk, tap_sum, 0)
    stat = sums_start(
        1,
        [
            row_of(jnp.sum(gpre_ref[...] * normed_ref[...], axis=1, keepdims=True)),
            row_of(jnp.sum(gpre_ref[...], axis=1, keepdims=True)),
        ],
    )

    def finish(kind, out_stage):
        arrived(back[kind])
        block = partial[kind][c, zh, slot_own].astype(F32) + landing[4][kind][0].astype(F32)
        first, second = block[:own], block[own:]
        staged(out_stage, jnp.where(c == 0, second, first))
        return jnp.where(c == 0, first, second)

    mine, swaps = [None] * 3, [None] * 3
    ends = ((ys_t, yr_t), (ys_a, yr_a), (ys_b, yr_b))
    for kind in (1, 2):
        mine[kind] = finish(kind, ends[kind][0])
        swaps[kind] = trade(1, kind, *ends[kind])
    stat = sums_middle(1, stat)
    mine[0] = finish(0, ends[0][0])
    swaps[0] = trade(1, 0, *ends[0])
    sums = sums_end(1, stat)

    scale = lax.rsqrt(count)
    chan_gain, chan_shift = sums[:, 0:chans], sums[:, stride : stride + chans]
    dgain[...] = scale * chan_gain
    dshift[...] = scale * chan_shift
    shift_sum = group_column(gain_row * chan_shift) / group_count
    gain_sum = group_column(gain_row * chan_gain) / group_count
    result = og[...].astype(F32) + rstd * (
        gain_column * gpre_ref[...] - shift_sum - normed_ref[...] * gain_sum
    )
    gi[...] = jnp.where(live, result, 0.0).astype(BF)

    for kind in (1, 2, 0):
        arrived(swaps[kind])
    theirs = [pair[1][0:own].astype(F32) for pair in ends]
    side_s = jnp.concatenate(mine[1:], axis=1), jnp.concatenate(theirs[1:], axis=1)
    for out, (a, b), wide in ((dws, side_s, sw), (dwt, (mine[0], theirs[0]), tw)):
        whole = jnp.concatenate([jnp.where(c == 0, a, b), jnp.where(c == 0, b, a)], axis=1)
        out[...] = scale * whole[:, 0:wide]

    for copy in pending:
        copy.wait_send()
    frame_sent(og_pair)
    for pair in (act_pair, gs_pair):
        strip_sent(pair)


def hand_over(*refs):
    for source, target in zip(refs[:5], refs[5:]):
        target[...] = source[...].reshape(target.shape)


def fused(latents, out_grad, w_spatial, w_temporal, norm_gain, norm_shift, heights):
    chans, cells = latents.shape[1:]
    own, sw = w_spatial.shape
    tw = w_temporal.shape[1]
    pad = -(-own // 16) * 16
    th = -(-tw // 256) * 128
    sh = -(-sw // 256) * 128
    kinds = (th, sh - 128, 128)
    sp, tp = 2 * sh, 2 * th
    wide = -(-chans // 128) * 128

    scratch = (
        [pltpu.VMEM((2, 2, 8, 2 * own, kind), BF) for _ in range(2) for kind in kinds]
        + [
            pltpu.VMEM(lead + (2 * own, kind), BF)
            for lead in ((2, 8), (2, 4), (2, 2), (2, 1), (1,))
            for kind in kinds
        ]
        + [pltpu.VMEM((pad, kind), BF) for _ in range(4) for kind in kinds]
        + [
            pltpu.VMEM((2, chans, cells), BF),
            pltpu.VMEM((3 * chans + tp - tw, cells), BF),
            pltpu.VMEM((2, 2, chans, cells // 2), BF),
            pltpu.VMEM((2, 2, chans, cells // 2), BF),
            pltpu.VMEM((chans, 2 * cells), F32),
            pltpu.VMEM((9 * chans + sp - sw, cells), BF),
            pltpu.VMEM((9 * chans, 2 * cells), F32),
            pltpu.VMEM((chans, cells), F32),
        ]
        + [pltpu.VMEM((chans, cells), F32)] * 4
        + [
            pltpu.VMEM((2, 2, 1, 3 * wide), F32),
            pltpu.VMEM((2, 8, 1, 3 * wide), F32),
            pltpu.VMEM((2, 4, 1, 3 * wide), F32),
            pltpu.VMEM((chans, chans), F32),
            pltpu.VMEM((chans, chans), F32),
        ]
        + [pltpu.SemaphoreType.DMA((3, 8))] * 4
        + [pltpu.SemaphoreType.DMA((2,))] * 2
        + [pltpu.SemaphoreType.DMA((2, 2))] * 2
        + [pltpu.SemaphoreType.DMA((2, 12))] * 2
        + [pltpu.SemaphoreType.DMA((2, 3))] * 2
    )
    vmem = pl.BlockSpec(memory_space=pltpu.VMEM)
    outs = pl.pallas_call(
        whole_kernel,
        out_shape=(
            jax.ShapeDtypeStruct((chans, cells), BF),
            jax.ShapeDtypeStruct((own, sw), F32),
            jax.ShapeDtypeStruct((own, tw), F32),
            jax.ShapeDtypeStruct((1, chans), F32),
            jax.ShapeDtypeStruct((1, chans), F32),
        ),
        in_specs=[vmem] * 6 + [pl.BlockSpec(memory_space=pltpu.SMEM)],
        out_specs=(vmem,) * 5,
        scratch_shapes=scratch,
        compiler_params=pltpu.CompilerParams(
            collective_id=0, has_side_effects=True, vmem_limit_bytes=56 * 1024 * 1024
        ),
    )(
        latents[0], out_grad[0], w_spatial, w_temporal, norm_gain, norm_shift, heights
    )
    shapes = [outs[0].shape, outs[1].shape, outs[2].shape, (chans,), (chans,)]
    results = pl.pallas_call(
        hand_over,
        out_shape=tuple(
            jax.ShapeDtypeStruct(shape, out.dtype) for shape, out in zip(shapes, outs)
        ),
        in_specs=[vmem] * 5,
        out_specs=(vmem,) * 5,
    )(*outs)
    return (results[0][None],) + tuple(results[1:])


def solution(mesh):
    in_specs = (
        P("frame", None, "tile"),
        P("frame", None, "tile"),
        P("tile", "frame"),
        P("tile", "frame"),
        P(),
        P(),
        P("tile"),
    )
    out_specs = (P("frame", None, "tile"), P("tile", "frame"), P("tile", "frame"), P(), P())
    fits = mesh.shape["frame"] == 4 and mesh.shape["tile"] == 8
    return jax.shard_map(
        fused if fits else local, mesh=mesh, in_specs=in_specs, out_specs=out_specs, check_vma=False
    )
```
